512 devices in a mesh: wide: 128 (over z, x, core), narrow: 4 (over y).
Axes of the slice: x: 4, y: 4, z: 16, core: 2. Of those that a mesh axis runs over, the one named last changes fastest.
Arguments:
- position: float32 [3, 524288], P(None, ('wide', 'narrow')), may hold values from -6 to 6
- velocity: float32 [3, 524288], P(None, ('wide', 'narrow')), may hold values from -6 to 6
- mass: float32 [524288], P(('wide', 'narrow')), may hold values from 0.5 to 2
- energy: float32 [524288], P(('wide', 'narrow')), may hold values from 0.5 to 2
- smoothing: float32 [524288], P(('wide', 'narrow')), may hold values from 1.5 to 3
- local_near: int32 [4096], P(('wide', 'narrow')), may hold values from 0 to 7
- dens_block: int32 [4096], P(('wide', 'narrow')), may hold values from 0 to 7
- dens_dest: int32 [4096, 1], P(('wide', 'narrow')), may hold values from 0 to 3; in each aligned block of 8 rows (0 to 7, 8 to 15, ...) at most 6 rows name the same one
- dens_near: int32 [4096, 2], P(('wide', 'narrow')), may hold values from 0 to 7
- force_block: int32 [65536], P(('wide', 'narrow')), may hold values from 0 to 7
- force_dest: int32 [65536, 1], P(('wide', 'narrow')), may hold values from 0 to 127; in each aligned block of 128 rows (0 to 127, 128 to 255, ...) at most 3 rows name the same one
- force_near: int32 [65536, 2], P(('wide', 'narrow')), may hold values from 0 to 7
Outputs:
- density: float32 [524288], P(('wide', 'narrow'))
- accel: float32 [3, 524288], P(None, ('wide', 'narrow'))
- energy_rate: float32 [524288], P(('wide', 'narrow'))
The draws below stay inside these ranges and needn't reach their ends.
Inputs may be any that keep to these rules, and one draw needn't show every extreme that they name: `dens_dest`: among the 8 rows of one device no narrow index is named by more than 6 rows; some index is named exactly 6 times by the rows of some device. `force_dest`: among the 128 rows of one device no wide index is named by more than 3 rows; some index is named exactly 3 times by the rows of some device.
All inputs are finite; a program needn't handle non-finite values.
Results may differ from the reference program's by a relative error of at most 0.0003.
Values sent between devices are 32-bit elements; how exact they have to be, the bound alone decides.
A program may use at most 64 MiB of HBM per device.

```python
import math
import jax
import jax.numpy as jnp
import numpy as np
from jax import lax

BLK = 128
NB = 8
NL = 2
PASSES = 3
XN = 8
XW = 128
CAPN = 6
CAPW = 3
TOTAL = 524288
N_WIDE = 128
N_NARROW = 4


def plant(entries, own_key, low, largest):
    dims = entries.shape
    spot = [jax.random.randint(jax.random.fold_in(own_key, axis), (), 0, dims[axis]) for axis in range(len(dims))]
    entries = entries.at[tuple(spot)].set(low)
    longest = dims.index(max(dims))
    spot[longest] = (spot[longest] + 1) % dims[longest]
    return entries.at[tuple(spot)].set(largest)


def block_scale(own_key, extent, pieces, low, top_value):
    gain, own = 1.0, jax.random.fold_in(own_key, 6)
    for dim, parts in pieces:
        steps = jnp.exp(jax.random.uniform(jax.random.fold_in(own, dim), (parts,), jnp.float32, low / len(pieces), top_value / len(pieces)))
        gain = gain * jnp.repeat(steps, extent[dim] // parts).reshape([-1 if axis == dim else 1 for axis in range(len(extent))])
    return gain


def deal_out(own_key, own, number, rows, amount, top, reach, skew):
    ranking = jax.random.permutation(own_key, amount)
    heavy_load, usual = load_shares(amount, rows * top, reach, skew, True), load_shares(amount, rows * top, reach, skew, False)
    places = jnp.arange(amount)

    def named(lengths, rotation):
        used = int((lengths > 0).sum())
        fixed = max(1, used // 4)
        shifted = fixed + (places - fixed + rotation * (used - fixed)) % max(1, amount - fixed)
        return jnp.zeros((amount,), jnp.int32).at[ranking[jnp.where(places < fixed, places, shifted)]].set(jnp.asarray(lengths, jnp.int32))

    lengths = jnp.where(number % 4 == 0, named(heavy_load, number // 4), named(usual, number - number // 4 - 1))
    mixed = jax.random.permutation(jax.random.fold_in(own, 3), amount)
    donor, taker = mixed[0:amount // 2 * 2:2], mixed[1:amount // 2 * 2:2]
    room = jnp.minimum(lengths[donor] - 1, reach - lengths[taker]) // 2
    room = jnp.where((donor == ranking[0]) | (taker == ranking[0]) | (lengths[taker] == 0), 0, jnp.maximum(room, 0))
    shifted = jax.random.randint(jax.random.fold_in(own, 4), (amount // 2,), 0, 1 << 20) % (room + 1)
    lengths = lengths.at[donor].add(-shifted).at[taker].add(shifted)
    items = jnp.searchsorted(jnp.cumsum(lengths), jnp.arange(rows * top), side="right").astype(jnp.int32)
    grid = items.reshape(top, rows).T
    grid = grid[jax.random.permutation(jax.random.fold_in(own, 1), rows)]
    rotation = jax.random.randint(jax.random.fold_in(own, 2), (rows, 1), 0, top)
    return jnp.take_along_axis(grid, (jnp.arange(top)[None, :] + rotation) % top, axis=1)


def load_shares(number_of, total, bound, lean, full):
    portions = [(1 << 20) // math.isqrt(standing ** lean) + 1 for standing in range(1, number_of + 1)]
    largest = bound if full else min(bound, max(-(-total // number_of), total * portions[0] // sum(portions)))
    least = 1 if total - largest >= number_of - 1 else 0
    counts, rest = [largest] + [least] * (number_of - 1), total - largest - least * (number_of - 1)
    while rest > 0:
        free = [i for i in range(1, number_of) if counts[i] < largest] or [i for i in range(1, number_of) if counts[i] < bound]
        whole, remaining = sum([portions[i] for i in free]), rest
        for i in free:
            more = min(bound - counts[i], max(1, remaining * portions[i] // whole), rest)
            counts[i] = counts[i] + more
            rest = rest - more
    return np.array(counts)


def noise(rng, shape, scale, most, pieces=(), held_as=jnp.bfloat16):
    entries = jax.random.normal(rng, shape, jnp.float32) * scale
    if len(pieces) > 0:
        entries = block_scale(rng, shape, pieces, -0.22, 0.18) * entries
    return jnp.clip(entries, min=-most, max=most).astype(held_as)


def setup_inputs(seed: int = 0) -> dict:
    splits = jax.random.split(jax.random.key(seed), 13)
    position = noise(splits[0], (3, TOTAL), 1.0, 6.0, ((1, 512),), jnp.float32)
    velocity = noise(splits[1], (3, TOTAL), 1.0, 6.0, ((1, 512),), jnp.float32)
    mass = jnp.clip(jnp.exp(math.log(2.0) - 1.3862944 * jax.random.uniform(splits[2], (TOTAL,), jnp.float32) ** block_scale(splits[2], (TOTAL,), ((0, 512),), -0.2, 0.2)), 0.5, 2.0)
    energy = jnp.clip(jnp.exp(math.log(2.0) - 1.3862944 * jax.random.uniform(splits[3], (TOTAL,), jnp.float32) ** block_scale(splits[3], (TOTAL,), ((0, 512),), -0.2, 0.2)), 0.5, 2.0)
    smoothing = jnp.clip(jnp.exp(math.log(3.0) - 0.6931472 * jax.random.uniform(splits[4], (TOTAL,), jnp.float32) ** block_scale(splits[4], (TOTAL,), ((0, 512),), -0.2, 0.2)), 1.5, 3.0)
    local_near = plant(jax.random.randint(splits[5], (N_WIDE * N_NARROW * NB,), 0, NB), jax.random.fold_in(splits[5], 1), 0, NB - 1).astype(jnp.int32)
    dens_block = plant(jax.random.randint(splits[6], (N_WIDE * N_NARROW * XN,), 0, NB), jax.random.fold_in(splits[6], 1), 0, NB - 1).astype(jnp.int32)
    dens_dest_keys = jax.random.split(jax.random.fold_in(splits[7], 1), (N_WIDE * N_NARROW * XN) // XN)
    dens_dest_turns = jax.random.permutation(jax.random.fold_in(splits[7], 3), (N_WIDE * N_NARROW * XN) // XN)
    dens_dest = jax.vmap(lambda own, number: deal_out(jax.random.fold_in(splits[7], 2), own, number, XN, N_NARROW, 1, CAPN, 2))(dens_dest_keys, dens_dest_turns).reshape((N_WIDE * N_NARROW * XN, 1))
    dens_near = plant(jax.random.randint(splits[8], (N_WIDE * N_NARROW * XN, NL), 0, NB), jax.random.fold_in(splits[8], 1), 0, NB - 1).astype(jnp.int32)
    force_block = plant(jax.random.randint(splits[9], (N_WIDE * N_NARROW * XW,), 0, NB), jax.random.fold_in(splits[9], 1), 0, NB - 1).astype(jnp.int32)
    force_dest_keys = jax.random.split(jax.random.fold_in(splits[10], 1), (N_WIDE * N_NARROW * XW) // XW)
    force_dest_turns = jax.random.permutation(jax.random.fold_in(splits[10], 3), (N_WIDE * N_NARROW * XW) // XW)
    force_dest = jax.vmap(lambda own, number: deal_out(jax.random.fold_in(splits[10], 2), own, number, XW, N_WIDE, 1, CAPW, 2))(force_dest_keys, force_dest_turns).reshape((N_WIDE * N_NARROW * XW, 1))
    force_near = plant(jax.random.randint(splits[11], (N_WIDE * N_NARROW * XW, NL), 0, NB), jax.random.fold_in(splits[11], 1), 0, NB - 1).astype(jnp.int32)
    return dict(position=position, velocity=velocity, mass=mass, energy=energy, smoothing=smoothing, local_near=local_near, dens_block=dens_block, dens_dest=dens_dest, dens_near=dens_near, force_block=force_block, force_dest=force_dest, force_near=force_near)


kernel_norm = math.pi ** (-1.5)
target_count = 24.0
gamma_gas = 5.0 / 3.0

def density_tile(target, source):
    dist_sq = jnp.zeros((target.shape[0], target.shape[2], source.shape[2]), target.dtype)
    for comp in range(3):
        delta = target[:, comp, :, None] - source[:, comp, None, :]
        dist_sq = dist_sq + delta * delta
    width = target[:, 3, :, None]
    weight = jnp.exp(-dist_sq / (width * width)) * source[:, 3, None, :]
    return jnp.stack([lax.optimization_barrier(jnp.sum(weight, -1)), lax.optimization_barrier(jnp.sum(weight * dist_sq, -1))], axis=1)

def force_tile(target, source):
    deltas = [target[:, comp, :, None] - source[:, comp, None, :] for comp in range(3)]
    dist_sq = deltas[0] * deltas[0] + deltas[1] * deltas[1] + deltas[2] * deltas[2]
    vdot = (target[:, 3, :, None] - source[:, 3, None, :]) * deltas[0]
    vdot = vdot + (target[:, 4, :, None] - source[:, 4, None, :]) * deltas[1]
    vdot = vdot + (target[:, 5, :, None] - source[:, 5, None, :]) * deltas[2]
    width_i = target[:, 6, :, None]
    width_j = source[:, 7, None, :]
    grad_i = 2.0 * kernel_norm * jnp.exp(-dist_sq / (width_i * width_i)) / width_i ** 5
    grad_j = 2.0 * kernel_norm * jnp.exp(-dist_sq / (width_j * width_j)) / width_j ** 5
    mean_width = 0.5 * (width_i + width_j)
    approach = jnp.minimum(mean_width * vdot / (dist_sq + 0.01 * mean_width * mean_width), 0.0)
    sound_mean = 0.5 * (target[:, 9, :, None] + source[:, 10, None, :])
    rho_mean = 0.5 * (target[:, 7, :, None] + source[:, 8, None, :])
    visc = (-sound_mean * approach + 2.0 * approach * approach) / rho_mean
    grad_mean = 0.5 * (grad_i + grad_j)
    mass_j = source[:, 6, None, :]
    own_term = target[:, 8, :, None] * grad_i
    push = mass_j * (own_term + source[:, 9, None, :] * grad_j + visc * grad_mean)
    heat = -mass_j * (own_term + 0.5 * visc * grad_mean) * vdot
    return jnp.stack([lax.optimization_barrier(jnp.sum(push * deltas[0], -1)), lax.optimization_barrier(jnp.sum(push * deltas[1], -1)), lax.optimization_barrier(jnp.sum(push * deltas[2], -1)), lax.optimization_barrier(jnp.sum(heat, -1))], axis=1)

def grouped(kernel, target, source):
    items = target.shape[0]
    group = max((size for size in range(1, 17) if items % size == 0))
    if group == items:
        return kernel(target, source)
    shaped_t = target.reshape((items // group, group) + target.shape[1:])
    shaped_s = source.reshape((items // group, group) + source.shape[1:])
    result = lax.map(lambda pair: kernel(pair[0], pair[1]), (shaped_t, shaped_s))
    return result.reshape((items,) + result.shape[2:])

def join_blocks(picked):
    return picked.transpose(0, 2, 1, 3).reshape(picked.shape[0], picked.shape[2], picked.shape[1] * picked.shape[3])

def reference(position, velocity, mass, energy, smoothing, local_near, dens_block, dens_dest, dens_near, force_block, force_dest, force_near):
    devices = N_WIDE * N_NARROW

    def blocks_of(field):
        return field.reshape(field.shape[0], devices, NB, BLK).transpose(1, 2, 0, 3)
    pos_blocks = blocks_of(position)
    vel_blocks = blocks_of(velocity)
    mass_blocks = blocks_of(mass[None])
    energy_blocks = blocks_of(energy[None])
    width = blocks_of(smoothing[None])
    near_local = local_near.reshape(devices, NB)
    device_ids = jnp.arange(devices, dtype=jnp.int32)
    dens_owner = (device_ids // N_NARROW)[:, None] * N_NARROW + dens_dest.reshape(devices, XN)
    force_owner = force_dest.reshape(devices, XW) * N_NARROW + (device_ids % N_NARROW)[:, None]
    dens_rows = dens_block.reshape(devices, XN)
    dens_lists = dens_near.reshape(devices, XN, NL)
    force_rows = force_block.reshape(devices, XW)
    force_lists = force_near.reshape(devices, XW, NL)
    block_ids = jnp.arange(NB, dtype=jnp.int32)

    def sum_over(kernel, targets, sources, rows, owner, lists, width_out):

        def one_device(device):
            target = targets[device]
            local_src = join_blocks(jnp.stack([sources[device], sources[device][near_local[device]]], axis=1))
            local_part = grouped(kernel, target, local_src)
            remote_src = join_blocks(sources[owner[device][:, None], lists[device]])
            remote_part = grouped(kernel, target[rows[device]], remote_src)
            onehot = (block_ids[:, None] == rows[device][None, :]).astype(jnp.float32)
            added = jnp.dot(onehot, remote_part.reshape(remote_part.shape[0], -1), precision=lax.Precision.HIGHEST)
            return local_part + added.reshape(NB, width_out, BLK)
        return lax.map(one_device, device_ids)
    dens_source = jnp.concatenate([pos_blocks, mass_blocks], axis=2)
    total = width
    for step in range(PASSES):
        targets = jnp.concatenate([pos_blocks, width], axis=2)
        sums = sum_over(density_tile, targets, dens_source, dens_rows, dens_owner, dens_lists, 2)
        total = sums[:, :, 0:1]
        moment = sums[:, :, 1:2]
        if step + 1 < PASSES:
            ratio = jnp.log(kernel_norm * total / (target_count * mass_blocks))
            slope = 2.0 * moment / (width * width * total)
            width = width * jnp.exp(-ratio / (3.0 + slope))
    rho = kernel_norm * total / width ** 3
    press_coef = (gamma_gas - 1.0) * energy_blocks / rho
    sound = jnp.sqrt(gamma_gas * (gamma_gas - 1.0) * energy_blocks)
    force_target = jnp.concatenate([pos_blocks, vel_blocks, width, rho, press_coef, sound], axis=2)
    force_source = jnp.concatenate([pos_blocks, vel_blocks, mass_blocks, width, rho, press_coef, sound], axis=2)
    result = sum_over(force_tile, force_target, force_source, force_rows, force_owner, force_lists, 4)
    accel = result[:, :, 0:3].transpose(2, 0, 1, 3).reshape(3, TOTAL)
    energy_rate = result[:, :, 3].reshape(TOTAL)
    return (rho.reshape(TOTAL), accel, energy_rate)
```

```python
import functools
import math

import jax
import jax.numpy as jnp
from jax import lax
from jax.experimental import pallas as pl
from jax.experimental.pallas import tpu as pltpu
from jax.sharding import PartitionSpec as P

F32, BF16 = jnp.float32, jnp.bfloat16
MESH = pl.DeviceIdType.MESH

PASSES = 3
KERNEL_NORM = math.pi ** (-1.5)
TARGET_COUNT = 24.0
LOG2E = math.log2(math.e)

NB = 8
BLK = 128
NZ, NX, NC, NY = 16, 4, 2, 4
XN = 8
XW = 128
ITEMS = NB + XW
KF = 64

Z_ORDER = [0]
for _d in range(1, NZ // 2):
    Z_ORDER += [_d, -_d]
Z_ORDER.append(NZ // 2)
Z_PLACE = {d % NZ: p for p, d in enumerate(Z_ORDER)}
BATCHES = ((0, 1), (1, 5), (5, 9), (9, 13), (13, 16))


def remote(src, dst, send, recv, device):
    return pltpu.make_async_remote_copy(
        src_ref=src,
        dst_ref=dst,
        send_sem=send,
        recv_sem=recv,
        device_id=device,
        device_id_type=MESH,
    )


class Gather:
    def __init__(self, own, out, zs, zr, xs, xr, cs, cr, lsem):
        self.own, self.out = own, out
        self.zs, self.zr, self.xs, self.xr, self.cs, self.cr = zs, zr, xs, xr, cs, cr
        self.lsem = lsem
        w = lax.axis_index("wide")
        self.z, self.x, self.c = w // (NX * NC), (w // NC) % NX, w % NC
        self.sent = []

    def device(self, dz, dx, dc):
        z = (self.z + dz) % NZ
        x = (self.x + dx) % NX
        c = (self.c + dc) % NC
        return {"wide": (z * NX + x) * NC + c}

    def go(self, copy):
        copy.start()
        self.sent.append(copy)

    def start(self):
        self.local = pltpu.make_async_copy(self.own, self.out.at[0, 0, 0], self.lsem)
        self.local.start()
        for d in Z_ORDER[1:]:
            place = Z_PLACE[-d % NZ]
            self.go(
                remote(
                    self.own,
                    self.out.at[0, 0, place],
                    self.zs.at[place],
                    self.zr.at[place],
                    self.device(d, 0, 0),
                )
            )
        self.local.wait()
        self.forward_x(0)
        self.forward_core(0, 0)

    def wait_z(self, batch):
        for place in range(*BATCHES[batch]):
            if place > 0:
                remote(
                    self.own,
                    self.out.at[0, 0, place],
                    self.zs.at[place],
                    self.zr.at[place],
                    self.device(1, 0, 0),
                ).wait_recv()

    def part(self, core, x, batch):
        lo, hi = BATCHES[batch]
        return self.out.at[core, x, pl.ds(lo, hi - lo)]

    def x_copy(self, batch, k):
        j = NX - k
        return remote(
            self.part(0, 0, batch),
            self.part(0, j, batch),
            self.xs.at[j, batch],
            self.xr.at[j, batch],
            self.device(0, k, 0),
        )

    def forward_x(self, batch):
        for k in (2, 1, 3):
            self.go(self.x_copy(batch, k))

    def core_copy(self, x, batch):
        return remote(
            self.part(0, x, batch),
            self.part(1, x, batch),
            self.cs.at[x, batch],
            self.cr.at[x, batch],
            self.device(0, 0, 1),
        )

    def forward_core(self, x, batch):
        self.go(self.core_copy(x, batch))

    def z_step(self, batch):
        self.wait_z(batch)
        self.forward_x(batch)
        self.forward_core(0, batch)

    def x_step(self, batch):
        for k in (1, 3, 2):
            self.x_copy(batch, k).wait_recv()
            self.forward_core(NX - k, batch)

    def finish(self):
        for batch in range(len(BATCHES)):
            for x in range(NX):
                self.core_copy(x, batch).wait_recv()
        for copy in self.sent:
            copy.wait_send()


def first_sums(item, target, sources, slope, r2_ref, mx_ref, tot_ref, mom_ref):
    tot = mom = 0.0
    for s, source in enumerate(sources):
        cols = source.T
        r2 = 0.0
        for q in range(3):
            delta = target[q : q + 1] - cols[:, q : q + 1]
            r2 = r2 + delta * delta
        mass = jnp.broadcast_to(cols[:, 6:7], (BLK, BLK))
        r2_ref[item, pl.ds(s * BLK, BLK)] = r2
        mx_ref[item, pl.ds(s * BLK, BLK)] = mass
        weight = jnp.exp2(r2 * slope) * mass
        tot = tot + jnp.sum(weight, axis=0, keepdims=True)
        mom = mom + jnp.sum(weight * r2, axis=0, keepdims=True)
    tot_ref[pl.ds(item, 1)] = tot
    mom_ref[pl.ds(item, 1)] = mom


def next_sums(item, slope, r2_ref, mx_ref, tot_ref, mom_ref):
    r2 = r2_ref[item]
    weight = jnp.exp2(r2 * slope) * mx_ref[item]
    tot_ref[pl.ds(item, 1)] = jnp.sum(weight, axis=0, keepdims=True)
    mom_ref[pl.ds(item, 1)] = jnp.sum(weight * r2, axis=0, keepdims=True)


def gather_kernel(
    near,
    dens_block,
    dens_source,
    own,
    mass,
    width_in,
    dens_rows,
    e_out,
    l_out,
    beside,
    r2_ref,
    mx_ref,
    tot_ref,
    mom_ref,
    slope_ref,
    late,
    ys,
    yr,
    *sems,
):
    half = len(sems) // 2
    early_gather = Gather(own, e_out, *sems[:half])
    late_gather = Gather(late, l_out, *sems[half:])
    n = lax.axis_index("narrow")

    barrier = pltpu.get_barrier_semaphore()
    partners = [{"narrow": (n + k) % NY} for k in range(1, NY)]
    partners += [early_gather.device(0, 0, 1)]
    partners += [early_gather.device(0, k, 0) for k in range(1, NX)]
    partners += [early_gather.device(d, 0, 0) for d in Z_ORDER[1:]]
    for device in partners:
        pl.semaphore_signal(barrier, inc=1, device_id=device, device_id_type=MESH)

    def set_slope(width):
        slope = -LOG2E / (width * width)
        for b in range(NB):
            slope_ref[b] = slope[b : b + 1]

    width = width_in[...]
    set_slope(width)

    def local_first(item, carry):
        target = own[item]
        first_sums(
            item,
            target,
            (target, own[near[item]]),
            slope_ref[item],
            r2_ref,
            mx_ref,
            tot_ref,
            mom_ref,
        )
        return carry

    lax.fori_loop(0, NB, local_first, 0)
    beside[pl.ds(0, NB)] = own[...]

    pl.semaphore_wait(barrier, len(partners))

    y_copies = []
    for k in range(1, NY):
        y_copies.append(
            remote(
                own,
                beside.at[pl.ds((NY - k) * NB, NB)],
                ys.at[NY - k],
                yr.at[NY - k],
                {"narrow": (n + k) % NY},
            )
        )
        y_copies[-1].start()
    early_gather.start()
    for copy in y_copies:
        copy.wait_recv()

    def export_first(e, carry):
        block = dens_block[e]
        first_sums(
            NB + e,
            own[block],
            (beside[dens_source[2 * e]], beside[dens_source[2 * e + 1]]),
            slope_ref[block],
            r2_ref,
            mx_ref,
            tot_ref,
            mom_ref,
        )
        return carry

    lax.fori_loop(0, XN, export_first, 0)

    def combined(ref):
        value = ref[pl.ds(0, NB)]
        for e in range(XN):
            value = value + dens_rows[e] * ref[pl.ds(NB + e, 1)]
        return value

    for step in range(PASSES):
        if step > 0:

            def local_next(item, carry):
                next_sums(item, slope_ref[item], r2_ref, mx_ref, tot_ref, mom_ref)
                return carry

            def export_next(e, carry):
                next_sums(NB + e, slope_ref[dens_block[e]], r2_ref, mx_ref, tot_ref, mom_ref)
                return carry

            lax.fori_loop(0, NB, local_next, 0)
            lax.fori_loop(0, XN, export_next, 0)
        total = combined(tot_ref)
        if step + 1 < PASSES:
            moment = combined(mom_ref)
            ratio = jnp.log(KERNEL_NORM * total / (TARGET_COUNT * mass[...]))
            bend = 2.0 * moment / (width * width * total)
            width = width * jnp.exp(-ratio / (3.0 + bend))
            set_slope(width)

    late[pl.ds(0, NB)] = width
    late[pl.ds(NB, NB)] = KERNEL_NORM * total / (width * width * width)
    late_gather.start()

    early_gather.z_step(1)
    early_gather.x_step(0)
    early_gather.z_step(2)
    early_gather.x_step(1)
    early_gather.z_step(3)
    late_gather.x_step(0)
    early_gather.x_step(2)
    early_gather.z_step(4)
    late_gather.z_step(1)
    early_gather.x_step(3)
    late_gather.z_step(2)
    late_gather.z_step(3)
    late_gather.z_step(4)
    early_gather.x_step(4)
    for batch in range(1, 5):
        late_gather.x_step(batch)
    early_gather.finish()
    late_gather.finish()
    for copy in y_copies:
        copy.wait_send()


def gather_call(near, dens_block, dens_source, own, mass, width, dens_rows):
    smem = pl.BlockSpec(memory_space=pltpu.SMEM)
    vmem = pl.BlockSpec(memory_space=pltpu.VMEM)
    batches = len(BATCHES)
    dma = pltpu.SemaphoreType.DMA
    per_gather = [dma((NZ,)), dma((NZ,))] + [dma((NX, batches))] * 4 + [dma]
    return pl.pallas_call(
        gather_kernel,
        out_shape=(
            jax.ShapeDtypeStruct((NC, NX, NZ, NB, 8, BLK), F32),
            jax.ShapeDtypeStruct((NC, NX, NZ, 2 * NB, BLK), F32),
        ),
        in_specs=[smem] * 3 + [vmem] * 4,
        out_specs=(pl.BlockSpec(memory_space=pl.ANY),) * 2,
        scratch_shapes=[
            pltpu.VMEM((NY * NB, 8, BLK), F32),
            pltpu.VMEM((NB + XN, 2 * BLK, BLK), F32),
            pltpu.VMEM((NB + XN, 2 * BLK, BLK), F32),
            pltpu.VMEM((NB + XN, BLK), F32),
            pltpu.VMEM((NB + XN, BLK), F32),
            pltpu.VMEM((NB, 1, BLK), F32),
            pltpu.VMEM((2 * NB, BLK), F32),
            dma((NY,)),
            dma((NY,)),
        ]
        + per_gather * 2,
        compiler_params=pltpu.CompilerParams(
            collective_id=0, has_side_effects=True, vmem_limit_bytes=32 * 2**20
        ),
        name="density_and_gather",
    )(near, dens_block, dens_source, own, mass, width, dens_rows)


def split_two(value):
    high = value.astype(BF16).astype(F32)
    return high, value - high


def split_three(value):
    high, rest = split_two(value)
    return (high,) + split_two(rest)


def target_features(tile):
    row = lax.broadcasted_iota(jnp.int32, tile.shape, 0)
    swapped = jnp.where(row < 3, pltpu.roll(tile, 5, 0), pltpu.roll(tile, 3, 0))
    squares = jnp.sum(jnp.where(row < 3, tile * tile, 0.0), axis=0, keepdims=True)
    crosses = jnp.sum(jnp.where(row < 3, tile * swapped, 0.0), axis=0, keepdims=True)
    distance = jnp.where(row < 3, -2.0 * tile, jnp.where(row == 6, 1.0, 0.0))
    approach = jnp.where(row < 6, -40.0 * swapped, jnp.where(row == 7, 40.0, 0.0))
    outs = []
    for factor, constant in ((distance, squares), (approach, 40.0 * crosses)):
        h, m, l = split_three(factor)
        ch, cm, cl = split_three(constant)
        constants = jnp.where(row == 0, ch, jnp.where(row == 1, cm, jnp.where(row == 2, cl, 0.0)))
        full = jnp.concatenate([h, m, l, h, m, h, constants] + [jnp.zeros_like(h)] * 9, axis=0)
        outs.append(full.T)
    return jnp.concatenate(outs, axis=0).astype(BF16)[:, :KF]


T_SQ, T_CROSS, T_EXP, T_SCALE, T_WIDTH, T_SOUND, T_RHO, T_PRESS = range(8)


def slot_table(tab_ref, slot, tiles_ref, late_ref):
    def column(q):
        return tiles_ref[slot, pl.ds(q, NB, stride=8)]

    x, y, z, vx, vy, vz = (column(q) for q in range(6))
    energy = column(7)
    width = late_ref[slot, pl.ds(0, NB)]
    rho = late_ref[slot, pl.ds(NB, NB)]
    tab_ref[slot, T_SQ] = x * x + y * y + z * z
    tab_ref[slot, T_CROSS] = x * vx + y * vy + z * vz
    tab_ref[slot, T_EXP] = -LOG2E / (width * width)
    tab_ref[slot, T_SCALE] = math.log2(2.0 * KERNEL_NORM) - 5.0 * jnp.log2(width)
    tab_ref[slot, T_WIDTH] = 0.05 * width
    tab_ref[slot, T_SOUND] = jnp.sqrt((10.0 / 9.0) * energy)
    tab_ref[slot, T_RHO] = 8.0 * rho
    tab_ref[slot, T_PRESS] = (2.0 / 3.0) * energy / rho


TARGET_VALUES = (T_EXP, T_SCALE, T_WIDTH, T_SOUND, T_RHO, T_PRESS)


def force_kernel(
    blk,
    sa,
    sb,
    tiles_ref,
    late_ref,
    rho_out,
    acc_out,
    heat_out,
    tab_ref,
    tl_ref,
    tg_ref,
    acc_ref,
    r0,
    r1,
    f0,
    f1,
    w0,
    w1,
):
    slots = tiles_ref.shape[0]

    def fill(slot, carry):
        slot_table(tab_ref, slot, tiles_ref, late_ref)
        return carry

    lax.fori_loop(0, slots, fill, 0)

    def prepare(b, carry):
        tl_ref[b] = target_features(tiles_ref[0, pl.ds(pl.multiple_of(b * 8, 8), 8)])
        for i, q in enumerate(TARGET_VALUES):
            tg_ref[b, i] = jnp.broadcast_to(tab_ref[0, q, pl.ds(b, 1)], (BLK, BLK)).T
        acc_ref[b] = jnp.zeros((16, 2 * BLK), F32)
        return carry

    lax.fori_loop(0, NB, prepare, 0)
    f1[...] = jnp.zeros(f1.shape, BF16)
    w1[...] = jnp.zeros(w1.shape, BF16)

    def pick(i, q):
        a, b = sa[i], sb[i]
        return jnp.concatenate(
            [tab_ref[a // NB, q, pl.ds(a % NB, 1)], tab_ref[b // NB, q, pl.ds(b % NB, 1)]], axis=1
        )

    def products(i, r_ref, f_ref):
        a, b = sa[i], sb[i]
        raw = jnp.concatenate(
            [
                tiles_ref[s // NB, pl.ds(pl.multiple_of((s % NB) * 8, 8), 8)]
                for s in (a, b)
            ],
            axis=1,
        )
        row = lax.broadcasted_iota(jnp.int32, raw.shape, 0)
        cross = pick(i, T_CROSS)
        u = jnp.where(row < 6, raw, jnp.where(row == 6, pick(i, T_SQ), cross))
        h, m, l = split_three(u)
        feats = jnp.concatenate([h, h, h, m, m, l, jnp.ones_like(h), jnp.zeros_like(h)], axis=0)
        r_ref[...] = jnp.dot(tl_ref[blk[i]], feats.astype(BF16), preferred_element_type=F32)
        f = jnp.where(row == 6, 1.0, u) * raw[6:7]
        f_ref[...] = jnp.concatenate(split_two(f), axis=0).astype(BF16)

    def pairs(i, r_ref, w_ref):
        b = blk[i]
        exp_j, scale_j, width_j, sound_j, rho_j, press_j = (pick(i, q) for q in TARGET_VALUES)
        for g in range(8):
            r2 = r_ref[pl.ds(16 * g, 16)]
            vd = r_ref[pl.ds(BLK + 16 * g, 16)]

            def own(q):
                value = tg_ref[b, q, pl.ds(16 * g, 16)]
                return jnp.concatenate([value, value], axis=1)

            hs = own(2) + width_j
            nu = jnp.minimum(hs * vd * pl.reciprocal(r2 + hs * hs, approx=True), 0.0)
            visc = nu * (nu - (own(3) + sound_j)) * pl.reciprocal(own(4) + rho_j, approx=True)
            grad_i = jnp.exp2(r2 * own(0) + own(1))
            grad_j = jnp.exp2(r2 * exp_j + scale_j)
            first = own(5) * grad_i
            both = first + visc * (grad_i + grad_j)
            w_ref[pl.ds(16 * g, 16)] = (both + press_j * grad_j).astype(BF16)
            w_ref[pl.ds(BLK + 16 * g, 16)] = (both + first).astype(BF16)

    def reduce(i, f_ref, w_ref):
        b = blk[i]
        acc_ref[b] = acc_ref[b] + lax.dot_general(
            f_ref[...], w_ref[...], (((1,), (1,)), ((), ())), preferred_element_type=F32
        )

    products(0, r0, f0)

    def body(k, carry):
        i = 2 * k
        reduce(jnp.maximum(i - 1, 0), f1, w1)
        products(i + 1, r1, f1)
        pairs(i, r0, w0)
        reduce(i, f0, w0)
        products(jnp.minimum(i + 2, ITEMS - 1), r0, f0)
        pairs(i + 1, r1, w1)
        return carry

    lax.fori_loop(0, ITEMS // 2, body, 0)
    reduce(ITEMS - 1, f1, w1)

    rho_out[...] = late_ref[0, pl.ds(NB, NB)]
    for b in range(NB):
        tile = tiles_ref[0, pl.ds(8 * b, 8)]
        s = acc_ref[b]
        s = s[0:8] + s[8:16]
        push, heat = s[:, 0:BLK], s[:, BLK:]
        for q in range(3):
            acc_out[q, pl.ds(b, 1)] = tile[q : q + 1] * push[6:7] - push[q : q + 1]
        value = tab_ref[0, T_CROSS, pl.ds(b, 1)] * heat[6:7] + heat[7:8]
        for q in range(3):
            value = value - tile[3 + q : 4 + q] * heat[q : q + 1]
            value = value - tile[q : q + 1] * heat[3 + q : 4 + q]
        heat_out[pl.ds(b, 1)] = -0.5 * value


def force_call(blk, sa, sb, tiles, late):
    smem = pl.BlockSpec(memory_space=pltpu.SMEM)
    vmem = pl.BlockSpec(memory_space=pltpu.VMEM)
    slots = NC * NX * NZ
    return pl.pallas_call(
        force_kernel,
        out_shape=(
            jax.ShapeDtypeStruct((NB, BLK), F32),
            jax.ShapeDtypeStruct((3, NB, BLK), F32),
            jax.ShapeDtypeStruct((NB, BLK), F32),
        ),
        in_specs=[smem] * 3 + [vmem] * 2,
        out_specs=(vmem,) * 3,
        scratch_shapes=[
            pltpu.VMEM((slots, 8, NB, BLK), F32),
            pltpu.VMEM((NB, 2 * BLK, KF), BF16),
            pltpu.VMEM((NB, 6, BLK, BLK), F32),
            pltpu.VMEM((NB, 16, 2 * BLK), F32),
            pltpu.VMEM((2 * BLK, 2 * BLK), F32),
            pltpu.VMEM((2 * BLK, 2 * BLK), F32),
            pltpu.VMEM((16, 2 * BLK), BF16),
            pltpu.VMEM((16, 2 * BLK), BF16),
            pltpu.VMEM((2 * BLK, 2 * BLK), BF16),
            pltpu.VMEM((2 * BLK, 2 * BLK), BF16),
        ],
        compiler_params=pltpu.CompilerParams(vmem_limit_bytes=40 * 2**20),
        name="force",
    )(blk, sa, sb, tiles, late)


def on_device(
    position,
    velocity,
    mass,
    energy,
    smoothing,
    local_near,
    dens_block,
    dens_dest,
    dens_near,
    force_block,
    force_dest,
    force_near,
):
    fields = jnp.concatenate([position, velocity, mass[None], energy[None]], axis=0)
    own = fields.reshape(8, NB, BLK).transpose(1, 0, 2)
    blocks = jnp.arange(NB, dtype=jnp.int32)
    row = (dens_dest - lax.axis_index("narrow") + NY) % NY
    dens_rows = jnp.broadcast_to(
        (dens_block[:, None] == blocks[None, :]).astype(F32)[:, :, None], (XN, NB, BLK)
    )
    tiles, late = gather_call(
        local_near,
        dens_block,
        (row * NB + dens_near).reshape(-1),
        own,
        mass.reshape(NB, BLK),
        smoothing.reshape(NB, BLK),
        dens_rows,
    )
    w = lax.axis_index("wide")
    z, x, c = w // (NX * NC), (w // NC) % NX, w % NC
    there = force_dest[:, 0]
    dz = (there // (NX * NC) - z + NZ) % NZ
    place = jnp.where(dz == 0, 0, jnp.where(dz <= NZ // 2, 2 * dz - 1, 2 * (NZ - dz)))
    dx = ((there // NC) % NX - x + NX) % NX
    dc = (there % NC - c + NC) % NC
    slot = (dc * NX + dx) * NZ + place
    blk = jnp.concatenate([blocks, force_block])
    sa = jnp.concatenate([blocks, slot * NB + force_near[:, 0]])
    sb = jnp.concatenate([local_near, slot * NB + force_near[:, 1]])
    slots = NC * NX * NZ
    rho, accel, heat = force_call(
        blk, sa, sb, tiles.reshape(slots, 8 * NB, BLK), late.reshape(slots, 2 * NB, BLK)
    )
    return rho.reshape(NB * BLK), accel.reshape(3, NB * BLK), heat.reshape(NB * BLK)


def solution(mesh):
    both = ("wide", "narrow")
    in_specs = (
        P(None, both),
        P(None, both),
        P(both),
        P(both),
        P(both),
        P(both),
        P(both),
        P(both, None),
        P(both, None),
        P(both),
        P(both, None),
        P(both, None),
    )
    out_specs = (P(both), P(None, both), P(both))
    return jax.shard_map(
        on_device, mesh=mesh, in_specs=in_specs, out_specs=out_specs, check_vma=False
    )
```

```python
import functools
import math

import jax
import jax.numpy as jnp
from jax import lax
from jax.experimental import pallas as pl
from jax.experimental.pallas import tpu as pltpu
from jax.sharding import PartitionSpec as P

F32, BF16 = jnp.float32, jnp.bfloat16
MESH = pl.DeviceIdType.MESH

PASSES = 3
KERNEL_NORM = math.pi ** (-1.5)
TARGET_COUNT = 24.0
LOG2E = math.log2(math.e)

NB = 8
BLK = 128
NZ, NX, NC, NY = 16, 4, 2, 4
XN = 8
XW = 128
ITEMS = NB + XW
CHUNKS = 8
KF = 64

RELAY = 4
Z_ORDER = [0, 4, -4, 1, -1, 2, -2, 3, -3, 5, -5, 6, -6, 7, -7, 8]
Z_PLACE = {d % NZ: p for p, d in enumerate(Z_ORDER)}
BATCHES = ((0, 1), (1, 5), (5, 9), (9, 13), (13, 16))
FAR = Z_PLACE[NZ // 2]


def remote(src, dst, send, recv, device):
    return pltpu.make_async_remote_copy(
        src_ref=src,
        dst_ref=dst,
        send_sem=send,
        recv_sem=recv,
        device_id=device,
        device_id_type=MESH,
    )


AFTER_FIRST_PASS = ("Ez1",)
BEFORE_LAST_PASS = ("En0",)
AFTER_DENSITY = (
    "Ez2", "En1", "Ef0", "Ez3", "Ez4", "En2", "Ef1", "En3",
    "Lz1", "Lz2", "Ef2", "En4", "Ln0", "Lf0", "Lz3", "Lz4",
    "Ef3", "Ln1", "Lf1", "Ef4", "Ln2", "Lf2", "Ln3", "Lf3",
    "Ln4", "Lf4",
)


class Gather:
    def __init__(self, own, out, halved, zs, zr, xs, xr, cs, cr, lsem):
        self.own, self.out, self.halved = own, out, halved
        self.zs, self.zr, self.xs, self.xr, self.cs, self.cr = zs, zr, xs, xr, cs, cr
        self.lsem = lsem
        w = lax.axis_index("wide")
        self.z, self.x, self.c = w // (NX * NC), (w // NC) % NX, w % NC
        self.half = own.shape[0] // 2
        self.sent = []

    def device(self, dz, dx, dc):
        z = (self.z + dz + NZ) % NZ
        x = (self.x + dx + NX) % NX
        c = (self.c + dc) % NC
        return {"wide": (z * NX + x) * NC + c}

    def go(self, copy):
        copy.start()
        self.sent.append(copy)

    def halves(self, ref, side):
        return ref.at[pl.ds(side * self.half, self.half)]

    def z_copy(self, src, distance, hop, side=None):
        place = Z_PLACE[distance % NZ]
        dst, sem = self.out.at[0, 0, place], place
        if side is not None:
            src, dst = self.halves(src, side), self.halves(dst, side)
            sem = place + side
        return remote(src, dst, self.zs.at[sem], self.zr.at[sem], self.device(hop, 0, 0))

    def start(self):
        self.local = pltpu.make_async_copy(self.own, self.out.at[0, 0, 0], self.lsem)
        self.local.start()
        for d in Z_ORDER[1:]:
            if abs(d) <= RELAY:
                self.go(self.z_copy(self.own, -d, d))
        self.local.wait()
        self.forward_x(0)
        self.forward_core(0, 0)

    def wait_z(self, batch):
        for place in range(*BATCHES[batch]):
            if place == FAR:
                for side in range(2):
                    self.z_copy(self.own, NZ // 2, 1, side).wait_recv()
            elif place > 0:
                self.z_copy(self.own, Z_ORDER[place], 1).wait_recv()

    def relay_z(self):
        for sign, side in ((1, 0), (-1, 1)):
            src = self.out.at[0, 0, Z_PLACE[-sign * RELAY % NZ]]
            for k in range(1, NZ // 2 - RELAY):
                self.go(self.z_copy(src, -sign * (RELAY + k), sign * k))
            self.go(self.z_copy(src, NZ // 2, sign * (NZ // 2 - RELAY), side))

    def part(self, core, x, batch, side=None):
        lo, hi = BATCHES[batch]
        if side is None:
            return self.out.at[core, x, pl.ds(lo, hi - lo)]
        return self.out.at[core, x, pl.ds(lo, hi - lo), pl.ds(side * self.half, self.half)]

    def x_copy(self, batch, k):
        j = NX - k
        return remote(
            self.part(0, 0, batch),
            self.part(0, j, batch),
            self.xs.at[j, batch],
            self.xr.at[j, batch],
            self.device(0, k, 0),
        )

    def x_relay(self, batch, side):
        sign = 1 - 2 * side
        sem = 2 * side
        return remote(
            self.part(0, (NX - sign) % NX, batch, side),
            self.part(0, 2, batch, side),
            self.xs.at[sem, batch],
            self.xr.at[sem, batch],
            self.device(0, sign, 0),
        )

    def forward_x(self, batch):
        for k in (1, 3) if self.halved else (2, 1, 3):
            self.go(self.x_copy(batch, k))

    def core_copy(self, x, batch):
        return remote(
            self.part(0, x, batch),
            self.part(1, x, batch),
            self.cs.at[x, batch],
            self.cr.at[x, batch],
            self.device(0, 0, 1),
        )

    def forward_core(self, x, batch):
        self.go(self.core_copy(x, batch))

    def z_step(self, batch):
        self.wait_z(batch)
        if batch == 1:
            self.relay_z()
        self.forward_x(batch)
        self.forward_core(0, batch)

    def x_near(self, batch):
        for k, side in ((1, 0), (3, 1)):
            self.x_copy(batch, k).wait_recv()
            if self.halved:
                self.go(self.x_relay(batch, side))
        self.forward_core(1, batch)
        self.forward_core(3, batch)

    def x_far(self, batch):
        if self.halved:
            for side in range(2):
                self.x_relay(batch, side).wait_recv()
        else:
            self.x_copy(batch, 2).wait_recv()
        self.forward_core(2, batch)

    def finish(self):
        for batch in range(len(BATCHES)):
            for x in range(NX):
                self.core_copy(x, batch).wait_recv()
        for copy in self.sent:
            copy.wait_send()


def first_sums(item, target, sources, slope, r2_ref, mx_ref, tot_ref, mom_ref):
    tot = mom = 0.0
    for s, source in enumerate(sources):
        cols = source.T
        r2 = 0.0
        for q in range(3):
            delta = target[q : q + 1] - cols[:, q : q + 1]
            r2 = r2 + delta * delta
        mass = jnp.broadcast_to(cols[:, 6:7], (BLK, BLK))
        r2_ref[item, pl.ds(s * BLK, BLK)] = r2
        mx_ref[item, pl.ds(s * BLK, BLK)] = mass
        weight = jnp.exp2(r2 * slope) * mass
        tot = tot + jnp.sum(weight, axis=0, keepdims=True)
        mom = mom + jnp.sum(weight * r2, axis=0, keepdims=True)
    tot_ref[pl.ds(item, 1)] = tot
    mom_ref[pl.ds(item, 1)] = mom


def next_sums(item, slope, r2_ref, mx_ref, tot_ref, mom_ref):
    r2 = r2_ref[item]
    weight = jnp.exp2(r2 * slope) * mx_ref[item]
    tot_ref[pl.ds(item, 1)] = jnp.sum(weight, axis=0, keepdims=True)
    mom_ref[pl.ds(item, 1)] = jnp.sum(weight * r2, axis=0, keepdims=True)


def gather_kernel(
    near_in,
    dens_block_in,
    dens_dest_in,
    dens_near_in,
    position_in,
    velocity_in,
    mass_in,
    energy_in,
    width_in,
    e_out,
    l_out,
    beside,
    r2_ref,
    mx_ref,
    tot_ref,
    mom_ref,
    slope_ref,
    late,
    own,
    unit,
    near,
    dens_block,
    dens_dest,
    dens_near,
    position,
    velocity,
    mass,
    energy,
    first_width,
    ins,
    ys,
    yr,
    *sems,
):
    half = len(sems) // 2
    early_gather = Gather(own, e_out, True, *sems[:half])
    late_gather = Gather(late, l_out, False, *sems[half:])
    n = lax.axis_index("narrow")

    barrier = pltpu.get_barrier_semaphore()
    partners = [{"narrow": (n + k) % NY} for k in range(1, NY)]
    partners += [early_gather.device(0, 0, 1)]
    partners += [early_gather.device(0, k, 0) for k in range(1, NX)]
    partners += [early_gather.device(d, 0, 0) for d in Z_ORDER[1:] if abs(d) <= RELAY]
    for device in partners:
        pl.semaphore_signal(barrier, inc=1, device_id=device, device_id_type=MESH)

    incoming = [
        pltpu.make_async_copy(src, dst, ins.at[i])
        for i, (src, dst) in enumerate(
            (
                (near_in, near),
                (dens_block_in, dens_block),
                (dens_dest_in, dens_dest),
                (dens_near_in, dens_near),
                (position_in, position),
                (velocity_in, velocity),
                (mass_in, mass),
                (energy_in, energy),
                (width_in, first_width),
            )
        )
    ]
    for copy in incoming:
        copy.start()
    for copy in incoming:
        copy.wait()

    rows = lax.broadcasted_iota(jnp.int32, (NB, BLK), 0)
    for b in range(NB):
        for q in range(3):
            own[b, pl.ds(q, 1)] = position[pl.ds(q, 1), pl.ds(b * BLK, BLK)]
            own[b, pl.ds(3 + q, 1)] = velocity[pl.ds(q, 1), pl.ds(b * BLK, BLK)]
        own[b, pl.ds(6, 1)] = mass[pl.ds(b, 1)]
        own[b, pl.ds(7, 1)] = energy[pl.ds(b, 1)]
        unit[b] = jnp.where(rows == b, 1.0, 0.0)

    def set_slope(width):
        slope = -LOG2E / (width * width)
        for b in range(NB):
            slope_ref[b] = slope[b : b + 1]

    width = first_width[...]
    set_slope(width)

    def local_first(item, carry):
        target = own[item]
        first_sums(
            item,
            target,
            (target, own[near[item]]),
            slope_ref[item],
            r2_ref,
            mx_ref,
            tot_ref,
            mom_ref,
        )
        return carry

    lax.fori_loop(0, NB, local_first, 0)
    beside[pl.ds(pl.multiple_of(n * NB, NB), NB)] = own[...]

    pl.semaphore_wait(barrier, len(partners))

    y_copies = []
    for k in range(1, NY):
        y_copies.append(
            remote(
                own,
                beside.at[pl.ds(pl.multiple_of(n * NB, NB), NB)],
                ys.at[NY - k],
                yr.at[NY - k],
                {"narrow": (n + k) % NY},
            )
        )
        y_copies[-1].start()
    early_gather.start()
    for copy in y_copies:
        copy.wait_recv()

    def export_first(e, carry):
        block = dens_block[e]
        first_sums(
            NB + e,
            own[block],
            tuple(beside[dens_dest[e] * NB + dens_near[s, e]] for s in range(2)),
            slope_ref[block],
            r2_ref,
            mx_ref,
            tot_ref,
            mom_ref,
        )
        return carry

    lax.fori_loop(0, XN, export_first, 0)

    def follow(steps):
        for which, kind, batch in steps:
            gather = early_gather if which == "E" else late_gather
            {"z": gather.z_step, "n": gather.x_near, "f": gather.x_far}[kind](int(batch))

    def combined(ref):
        value = ref[pl.ds(0, NB)]
        for e in range(XN):
            value = value + unit[dens_block[e]] * ref[pl.ds(NB + e, 1)]
        return value

    follow(AFTER_FIRST_PASS)
    for step in range(PASSES):
        if step == PASSES - 1:
            follow(BEFORE_LAST_PASS)
        if step > 0:

            def local_next(item, carry):
                next_sums(item, slope_ref[item], r2_ref, mx_ref, tot_ref, mom_ref)
                return carry

            def export_next(e, carry):
                next_sums(NB + e, slope_ref[dens_block[e]], r2_ref, mx_ref, tot_ref, mom_ref)
                return carry

            lax.fori_loop(0, NB, local_next, 0)
            lax.fori_loop(0, XN, export_next, 0)
        total = combined(tot_ref)
        if step + 1 < PASSES:
            moment = combined(mom_ref)
            ratio = jnp.log(KERNEL_NORM * total / (TARGET_COUNT * mass[...]))
            bend = 2.0 * moment / (width * width * total)
            width = width * jnp.exp(-ratio / (3.0 + bend))
            set_slope(width)

    late[pl.ds(0, NB)] = width
    late[pl.ds(NB, NB)] = KERNEL_NORM * total / (width * width * width)
    late_gather.start()
    follow(AFTER_DENSITY)
    early_gather.finish()
    late_gather.finish()
    for copy in y_copies:
        copy.wait_send()


def gather_call(*args):
    batches = len(BATCHES)
    dma = pltpu.SemaphoreType.DMA
    per_gather = [dma((NZ + 1,)), dma((NZ + 1,))] + [dma((NX, batches))] * 4 + [dma]
    return pl.pallas_call(
        gather_kernel,
        out_shape=(
            jax.ShapeDtypeStruct((NC, NX, NZ, NB, 8, BLK), F32),
            jax.ShapeDtypeStruct((NC, NX, NZ, 2 * NB, BLK), F32),
        ),
        in_specs=[pl.BlockSpec(memory_space=pl.ANY)] * 9,
        out_specs=(pl.BlockSpec(memory_space=pl.ANY),) * 2,
        scratch_shapes=[
            pltpu.VMEM((NY * NB, 8, BLK), F32),
            pltpu.VMEM((NB + XN, 2 * BLK, BLK), F32),
            pltpu.VMEM((NB + XN, 2 * BLK, BLK), F32),
            pltpu.VMEM((NB + XN, BLK), F32),
            pltpu.VMEM((NB + XN, BLK), F32),
            pltpu.VMEM((NB, 1, BLK), F32),
            pltpu.VMEM((2 * NB, BLK), F32),
            pltpu.VMEM((NB, 8, BLK), F32),
            pltpu.VMEM((NB, NB, BLK), F32),
            pltpu.SMEM((NB,), jnp.int32),
            pltpu.SMEM((XN,), jnp.int32),
            pltpu.SMEM((XN,), jnp.int32),
            pltpu.SMEM((2, XN), jnp.int32),
            pltpu.VMEM((3, NB * BLK), F32),
            pltpu.VMEM((3, NB * BLK), F32),
            pltpu.VMEM((NB, BLK), F32),
            pltpu.VMEM((NB, BLK), F32),
            pltpu.VMEM((NB, BLK), F32),
            dma((9,)),
            dma((NY,)),
            dma((NY,)),
        ]
        + per_gather * 2,
        compiler_params=pltpu.CompilerParams(
            collective_id=0, has_side_effects=True, vmem_limit_bytes=62 * 2**20
        ),
        name="density_and_gather",
    )(*args)


def split_two(value):
    high = value.astype(BF16).astype(F32)
    return high, value - high


def split_three(value):
    high, rest = split_two(value)
    return (high,) + split_two(rest)


def target_features(tile, exp_i, scale_i):
    row = lax.broadcasted_iota(jnp.int32, tile.shape, 0)
    swapped = jnp.where(row < 3, pltpu.roll(tile, 5, 0), pltpu.roll(tile, 3, 0))
    squares = jnp.sum(jnp.where(row < 3, tile * tile, 0.0), axis=0, keepdims=True)
    crosses = jnp.sum(jnp.where(row < 3, tile * swapped, 0.0), axis=0, keepdims=True)
    distance = jnp.where(row < 3, -2.0 * tile, jnp.where(row == 6, 1.0, 0.0))
    approach = jnp.where(row < 6, -40.0 * swapped, jnp.where(row == 7, 40.0, 0.0))
    outs = []
    for factor, constant in (
        (distance, squares),
        (approach, 40.0 * crosses),
        (distance * exp_i, squares * exp_i + scale_i),
    ):
        h, m, l = split_three(factor)
        ch, cm, cl = split_three(constant)
        constants = jnp.where(row == 0, ch, jnp.where(row == 1, cm, jnp.where(row == 2, cl, 0.0)))
        full = jnp.concatenate([h, m, l, h, m, h, constants] + [jnp.zeros_like(h)] * 9, axis=0)
        outs.append(full.T)
    return jnp.concatenate(outs, axis=0).astype(BF16)[:, :KF]


T_SQ, T_CROSS, T_EXP, T_SCALE, T_WIDTH, T_SOUND, T_RHO, T_PRESS = range(8)


def slot_table(tab_ref, slot, tiles_ref, late_ref):
    def column(q):
        return tiles_ref[slot, pl.ds(q, NB, stride=8)]

    x, y, z, vx, vy, vz = (column(q) for q in range(6))
    energy = column(7)
    width = late_ref[slot, pl.ds(0, NB)]
    rho = late_ref[slot, pl.ds(NB, NB)]
    tab_ref[slot, T_SQ] = x * x + y * y + z * z
    tab_ref[slot, T_CROSS] = x * vx + y * vy + z * vz
    tab_ref[slot, T_EXP] = -LOG2E / (width * width)
    tab_ref[slot, T_SCALE] = math.log2(2.0 * KERNEL_NORM) - 5.0 * jnp.log2(width)
    tab_ref[slot, T_WIDTH] = 0.05 * width
    tab_ref[slot, T_SOUND] = jnp.sqrt((10.0 / 9.0) * energy)
    tab_ref[slot, T_RHO] = 8.0 * rho
    tab_ref[slot, T_PRESS] = (2.0 / 3.0) * energy / rho


TARGET_VALUES = (T_WIDTH, T_SOUND, T_RHO, T_PRESS)


def force_kernel(
    near_in,
    force_block_in,
    force_dest_in,
    force_near_in,
    tiles_in,
    late_in,
    rho_out,
    acc_out,
    heat_out,
    tab_ref,
    tiles_ref,
    late_ref,
    tl_ref,
    tg_ref,
    acc_ref,
    r0,
    r1,
    f0,
    f1,
    w0,
    w1,
    f2,
    near,
    force_block,
    force_dest,
    force_near,
    lists_v,
    lists,
    ins,
    tile_sems,
    late_sems,
):
    chunk = tiles_ref.shape[0] // CHUNKS
    incoming = [
        pltpu.make_async_copy(src, dst, ins.at[i])
        for i, (src, dst) in enumerate(
            (
                (near_in, near),
                (force_block_in, force_block),
                (force_dest_in, force_dest),
                (force_near_in, force_near),
            )
        )
    ]
    for copy in incoming:
        copy.start()

    loads = []
    for k in range(CHUNKS):
        part = pl.ds(k * chunk, chunk)
        loads.append(
            (
                pltpu.make_async_copy(tiles_in.at[part], tiles_ref.at[part], tile_sems.at[k]),
                pltpu.make_async_copy(late_in.at[part], late_ref.at[part], late_sems.at[k]),
            )
        )
        for copy in loads[-1]:
            copy.start()

    w = lax.axis_index("wide")
    for copy in incoming:
        copy.wait()
    there = force_dest[...]
    dz = ((there >> 3) - (w >> 3)) & 15
    dn = NZ - dz
    spot = jnp.where(
        dz <= NZ // 2,
        jnp.where(dz <= RELAY, 2 * dz + 1, 2 * dz - 1),
        jnp.where(dn <= RELAY, 2 * dn + 2, 2 * dn),
    )
    spot = jnp.where(dz == 0, 0, jnp.where(dz == RELAY, 1, jnp.where(dn == RELAY, 2, spot)))
    slot = (((there ^ w) & 1) * NX + (((there >> 1) - (w >> 1)) & 3)) * NZ + spot
    lists_v[:, pl.ds(0, XW)] = jnp.concatenate(
        [force_block[...], slot * NB + force_near[...]], axis=0
    )
    lists_v[:, pl.ds(XW, XW)] = jnp.zeros((3, XW), jnp.int32)
    to_scalars = pltpu.make_async_copy(lists_v, lists, ins.at[4])
    to_scalars.start()

    def fill(slot, carry):
        slot_table(tab_ref, slot, tiles_ref, late_ref)
        return carry

    def fill_chunk(k):
        for copy in loads[k]:
            copy.wait()
        lax.fori_loop(k * chunk, (k + 1) * chunk, fill, 0, unroll=4)

    fill_chunk(0)

    def prepare(b, carry):
        tl_ref[b] = target_features(
            tiles_ref[0, pl.ds(pl.multiple_of(b * 8, 8), 8)],
            tab_ref[0, T_EXP, pl.ds(b, 1)],
            tab_ref[0, T_SCALE, pl.ds(b, 1)],
        )
        for i, q in enumerate(TARGET_VALUES):
            tg_ref[b, i] = jnp.broadcast_to(tab_ref[0, q, pl.ds(b, 1)], (BLK, BLK)).T
        acc_ref[b] = jnp.zeros((16, 3 * BLK), F32)
        return carry

    lax.fori_loop(0, NB, prepare, 0)
    for k in range(1, CHUNKS):
        fill_chunk(k)
    to_scalars.wait()
    for b in range(NB):
        lists[0, XW + b] = b
        lists[1, XW + b] = b
        lists[2, XW + b] = near[b]
    f1[...] = jnp.zeros(f1.shape, BF16)
    w1[...] = jnp.zeros(w1.shape, BF16)

    def pick(i, q):
        a, b = lists[1, i], lists[2, i]
        return jnp.concatenate(
            [tab_ref[a >> 3, q, pl.ds(a & 7, 1)], tab_ref[b >> 3, q, pl.ds(b & 7, 1)]], axis=1
        )

    def products(i, r_ref, f_ref):
        a, b = lists[1, i], lists[2, i]
        raw = jnp.concatenate(
            [
                tiles_ref[s >> 3, pl.ds(pl.multiple_of((s & 7) * 8, 8), 8)]
                for s in (a, b)
            ],
            axis=1,
        )
        row = lax.broadcasted_iota(jnp.int32, raw.shape, 0)
        cross = pick(i, T_CROSS)
        u = jnp.where(row < 6, raw, jnp.where(row == 6, pick(i, T_SQ), cross))
        h, m, l = split_three(u)
        feats = jnp.concatenate([h, h, h, m, m, l, jnp.ones_like(h), jnp.zeros_like(h)], axis=0)
        r_ref[...] = jnp.dot(tl_ref[lists[0, i]], feats.astype(BF16), preferred_element_type=F32)
        f = jnp.where(row == 6, 1.0, u) * raw[6:7]
        f_ref[...] = jnp.concatenate(split_two(f), axis=0).astype(BF16)

    def pairs(i, r_ref, w_ref):
        b = lists[0, i]
        width_j, sound_j, rho_j, press_j = (pick(i, q) for q in TARGET_VALUES)
        exp_j, scale_j = pick(i, T_EXP), pick(i, T_SCALE)
        for g in range(8):
            r2 = r_ref[pl.ds(16 * g, 16)]
            vd = r_ref[pl.ds(BLK + 16 * g, 16)]

            def own(q):
                value = tg_ref[b, q, pl.ds(16 * g, 16)]
                return jnp.concatenate([value, value], axis=1)

            hs = own(0) + width_j
            nu = jnp.minimum(hs * vd * pl.reciprocal(r2 + hs * hs, approx=True), 0.0)
            visc = nu * (nu - (own(1) + sound_j)) * pl.reciprocal(own(2) + rho_j, approx=True)
            grad_i = jnp.exp2(r_ref[pl.ds(2 * BLK + 16 * g, 16)])
            grad_j = jnp.exp2(r2 * exp_j + scale_j)
            first = own(3) * grad_i
            both = first + visc * (grad_i + grad_j)
            w_ref[pl.ds(16 * g, 16)] = both.astype(BF16)
            w_ref[pl.ds(BLK + 16 * g, 16)] = first.astype(BF16)
            w_ref[pl.ds(2 * BLK + 16 * g, 16)] = (press_j * grad_j).astype(BF16)

    def reduce(i, f_ref, w_ref):
        b = lists[0, i]
        acc_ref[b] = acc_ref[b] + lax.dot_general(
            f_ref[...], w_ref[...], (((1,), (1,)), ((), ())), preferred_element_type=F32
        )

    products(0, r0, f0)

    def body(k, carry):
        i = 2 * k
        reduce(jnp.maximum(i - 1, 0), f1, w1)
        products(i + 1, r1, f1)
        pairs(i, r0, w0)
        products(jnp.minimum(i + 2, ITEMS - 1), r0, f2)
        reduce(i, f0, w0)
        f0[...] = f2[...]
        pairs(i + 1, r1, w1)
        return carry

    lax.fori_loop(0, ITEMS // 2, body, 0, unroll=17)
    reduce(ITEMS - 1, f1, w1)

    rho_out[...] = late_ref[0, pl.ds(NB, NB)]
    for b in range(NB):
        tile = tiles_ref[0, pl.ds(8 * b, 8)]
        s = acc_ref[b]
        s = s[0:8] + s[8:16]
        push, heat = s[:, 0:BLK] + s[:, 2 * BLK :], s[:, 0:BLK] + s[:, BLK : 2 * BLK]
        for q in range(3):
            acc_out[pl.ds(q, 1), pl.ds(b * BLK, BLK)] = tile[q : q + 1] * push[6:7] - push[q : q + 1]
        value = tab_ref[0, T_CROSS, pl.ds(b, 1)] * heat[6:7] + heat[7:8]
        for q in range(3):
            value = value - tile[3 + q : 4 + q] * heat[q : q + 1]
            value = value - tile[q : q + 1] * heat[3 + q : 4 + q]
        heat_out[pl.ds(b, 1)] = -0.5 * value


def force_call(*args):
    vmem = pl.BlockSpec(memory_space=pltpu.VMEM)
    slots = NC * NX * NZ
    return pl.pallas_call(
        force_kernel,
        out_shape=(
            jax.ShapeDtypeStruct((NB, BLK), F32),
            jax.ShapeDtypeStruct((3, NB * BLK), F32),
            jax.ShapeDtypeStruct((NB, BLK), F32),
        ),
        in_specs=[pl.BlockSpec(memory_space=pl.ANY)] * 6,
        out_specs=(vmem,) * 3,
        scratch_shapes=[
            pltpu.VMEM((slots, 8, NB, BLK), F32),
            pltpu.VMEM((slots, 8 * NB, BLK), F32),
            pltpu.VMEM((slots, 2 * NB, BLK), F32),
            pltpu.VMEM((NB, 3 * BLK, KF), BF16),
            pltpu.VMEM((NB, len(TARGET_VALUES), BLK, BLK), F32),
            pltpu.VMEM((NB, 16, 3 * BLK), F32),
            pltpu.VMEM((3 * BLK, 2 * BLK), F32),
            pltpu.VMEM((3 * BLK, 2 * BLK), F32),
            pltpu.VMEM((16, 2 * BLK), BF16),
            pltpu.VMEM((16, 2 * BLK), BF16),
            pltpu.VMEM((3 * BLK, 2 * BLK), BF16),
            pltpu.VMEM((3 * BLK, 2 * BLK), BF16),
            pltpu.VMEM((16, 2 * BLK), BF16),
            pltpu.SMEM((NB,), jnp.int32),
            pltpu.VMEM((1, XW), jnp.int32),
            pltpu.VMEM((1, XW), jnp.int32),
            pltpu.VMEM((2, XW), jnp.int32),
            pltpu.VMEM((3, 2 * XW), jnp.int32),
            pltpu.SMEM((3, 2 * XW), jnp.int32),
            pltpu.SemaphoreType.DMA((5,)),
            pltpu.SemaphoreType.DMA((CHUNKS,)),
            pltpu.SemaphoreType.DMA((CHUNKS,)),
        ],
        compiler_params=pltpu.CompilerParams(vmem_limit_bytes=62 * 2**20),
        name="force",
    )(*args)


def on_device(
    position,
    velocity,
    mass,
    energy,
    smoothing,
    local_near,
    dens_block,
    dens_dest,
    dens_near,
    force_block,
    force_dest,
    force_near,
):
    tiles, late = gather_call(
        local_near,
        dens_block,
        dens_dest.reshape(-1),
        dens_near.T,
        position,
        velocity,
        mass.reshape(NB, BLK),
        energy.reshape(NB, BLK),
        smoothing.reshape(NB, BLK),
    )
    slots = NC * NX * NZ
    rho, accel, heat = force_call(
        local_near,
        force_block.reshape(1, XW),
        force_dest.T,
        force_near.T,
        tiles.reshape(slots, 8 * NB, BLK),
        late.reshape(slots, 2 * NB, BLK),
    )
    return rho.reshape(NB * BLK), accel, heat.reshape(NB * BLK)


def solution(mesh):
    both = ("wide", "narrow")
    in_specs = (
        P(None, both),
        P(None, both),
        P(both),
        P(both),
        P(both),
        P(both),
        P(both),
        P(both, None),
        P(both, None),
        P(both),
        P(both, None),
        P(both, None),
    )
    out_specs = (P(both), P(None, both), P(both))
    return jax.shard_map(
        on_device, mesh=mesh, in_specs=in_specs, out_specs=out_specs, check_vma=False
    )
```

```python
import functools
import math

import jax
import jax.numpy as jnp
from jax import lax
from jax.experimental import pallas as pl
from jax.experimental.pallas import tpu as pltpu
from jax.sharding import PartitionSpec as P

F32, BF16 = jnp.float32, jnp.bfloat16
MESH = pl.DeviceIdType.MESH

PASSES = 3
KERNEL_NORM = math.pi ** (-1.5)
TARGET_COUNT = 24.0
LOG2E = math.log2(math.e)

NB = 8
BLK = 128
NZ, NX, NC, NY = 16, 4, 2, 4
XN = 8
XW = 128
ITEMS = NB + XW
CHUNKS = 8
KF = 64

RELAY = 4
Z_ORDER = [0, 4, -4, 1, -1, 2, -2, 3, -3, 5, -5, 6, -6, 7, -7, 8]
Z_PLACE = {d % NZ: p for p, d in enumerate(Z_ORDER)}
BATCHES = ((0, 1), (1, 5), (5, 9), (9, 13), (13, 16))
FAR = Z_PLACE[NZ // 2]


def remote(src, dst, send, recv, device):
    return pltpu.make_async_remote_copy(
        src_ref=src,
        dst_ref=dst,
        send_sem=send,
        recv_sem=recv,
        device_id=device,
        device_id_type=MESH,
    )


AFTER_FIRST_PASS = ("Ez1",)
BEFORE_LAST_PASS = ("En0",)
AFTER_DENSITY = (
    "Ez2", "En1", "Ef0", "Ez3", "Ez4", "En2", "Ef1", "En3",
    "Lz1", "Lz2", "Ef2", "En4", "Ln0", "Lf0", "Lz3", "Lz4",
    "Ef3", "Ln1", "Lf1", "Ef4", "Ln2", "Lf2", "Ln3", "Lf3",
    "Ln4", "Lf4",
)


UNROLL_FIRST = 4
UNROLL_NEXT = 8


class Gather:
    def __init__(self, own, out, halved, zs, zr, xs, xr, cs, cr, lsem):
        self.own, self.out, self.halved = own, out, halved
        self.zs, self.zr, self.xs, self.xr, self.cs, self.cr = zs, zr, xs, xr, cs, cr
        self.lsem = lsem
        w = lax.axis_index("wide")
        self.z, self.x, self.c = w // (NX * NC), (w // NC) % NX, w % NC
        self.half = own.shape[0] // 2
        self.sent = []

    def device(self, dz, dx, dc):
        z = (self.z + dz + NZ) % NZ
        x = (self.x + dx + NX) % NX
        c = (self.c + dc) % NC
        return {"wide": (z * NX + x) * NC + c}

    def go(self, copy):
        copy.start()
        self.sent.append(copy)

    def halves(self, ref, side):
        return ref.at[pl.ds(side * self.half, self.half)]

    def z_copy(self, src, distance, hop, side=None):
        place = Z_PLACE[distance % NZ]
        dst, sem = self.out.at[0, 0, place], place
        if side is not None:
            src, dst = self.halves(src, side), self.halves(dst, side)
            sem = place + side
        return remote(src, dst, self.zs.at[sem], self.zr.at[sem], self.device(hop, 0, 0))

    def start(self):
        self.local = pltpu.make_async_copy(self.own, self.out.at[0, 0, 0], self.lsem)
        self.local.start()
        for d in Z_ORDER[1:]:
            if abs(d) <= RELAY:
                self.go(self.z_copy(self.own, -d, d))
        self.local.wait()
        self.forward_x(0)
        self.forward_core(0, 0)

    def wait_z(self, batch):
        for place in range(*BATCHES[batch]):
            if place == FAR:
                for side in range(2):
                    self.z_copy(self.own, NZ // 2, 1, side).wait_recv()
            elif place > 0:
                self.z_copy(self.own, Z_ORDER[place], 1).wait_recv()

    def relay_z(self):
        for sign, side in ((1, 0), (-1, 1)):
            src = self.out.at[0, 0, Z_PLACE[-sign * RELAY % NZ]]
            for k in range(1, NZ // 2 - RELAY):
                self.go(self.z_copy(src, -sign * (RELAY + k), sign * k))
            self.go(self.z_copy(src, NZ // 2, sign * (NZ // 2 - RELAY), side))

    def part(self, core, x, batch, side=None):
        lo, hi = BATCHES[batch]
        if side is None:
            return self.out.at[core, x, pl.ds(lo, hi - lo)]
        return self.out.at[core, x, pl.ds(lo, hi - lo), pl.ds(side * self.half, self.half)]

    def x_copy(self, batch, k):
        j = NX - k
        return remote(
            self.part(0, 0, batch),
            self.part(0, j, batch),
            self.xs.at[j, batch],
            self.xr.at[j, batch],
            self.device(0, k, 0),
        )

    def x_relay(self, batch, side):
        sign = 1 - 2 * side
        sem = 2 * side
        return remote(
            self.part(0, (NX - sign) % NX, batch, side),
            self.part(0, 2, batch, side),
            self.xs.at[sem, batch],
            self.xr.at[sem, batch],
            self.device(0, sign, 0),
        )

    def forward_x(self, batch):
        for k in (1, 3) if self.halved else (2, 1, 3):
            self.go(self.x_copy(batch, k))

    def core_copy(self, x, batch):
        return remote(
            self.part(0, x, batch),
            self.part(1, x, batch),
            self.cs.at[x, batch],
            self.cr.at[x, batch],
            self.device(0, 0, 1),
        )

    def forward_core(self, x, batch):
        self.go(self.core_copy(x, batch))

    def z_step(self, batch):
        self.wait_z(batch)
        if batch == 1:
            self.relay_z()
        self.forward_x(batch)
        self.forward_core(0, batch)

    def x_near(self, batch):
        for k, side in ((1, 0), (3, 1)):
            self.x_copy(batch, k).wait_recv()
            if self.halved:
                self.go(self.x_relay(batch, side))
        self.forward_core(1, batch)
        self.forward_core(3, batch)

    def x_far(self, batch):
        if self.halved:
            for side in range(2):
                self.x_relay(batch, side).wait_recv()
        else:
            self.x_copy(batch, 2).wait_recv()
        self.forward_core(2, batch)

    def finish(self):
        for batch in range(len(BATCHES)):
            for x in range(NX):
                self.core_copy(x, batch).wait_recv()
        for copy in self.sent:
            copy.wait_send()


def first_sums(item, target, sources, slope, r2_ref, mx_ref, tot_ref, mom_ref):
    tot = mom = 0.0
    for s, source in enumerate(sources):
        cols = source.T
        r2 = 0.0
        for q in range(3):
            delta = target[q : q + 1] - cols[:, q : q + 1]
            r2 = r2 + delta * delta
        mass = jnp.broadcast_to(cols[:, 6:7], (BLK, BLK))
        r2_ref[item, pl.ds(s * BLK, BLK)] = r2
        mx_ref[item, pl.ds(s * BLK, BLK)] = mass
        weight = jnp.exp2(r2 * slope) * mass
        tot = tot + jnp.sum(weight, axis=0, keepdims=True)
        mom = mom + jnp.sum(weight * r2, axis=0, keepdims=True)
    tot_ref[pl.ds(item, 1)] = tot
    mom_ref[pl.ds(item, 1)] = mom


def next_sums(item, slope, r2_ref, mx_ref, tot_ref, mom_ref):
    r2 = r2_ref[item]
    weight = jnp.exp2(r2 * slope) * mx_ref[item]
    tot_ref[pl.ds(item, 1)] = jnp.sum(weight, axis=0, keepdims=True)
    mom_ref[pl.ds(item, 1)] = jnp.sum(weight * r2, axis=0, keepdims=True)


def gather_kernel(
    near_in,
    dens_block_in,
    dens_dest_in,
    dens_near_in,
    position_in,
    velocity_in,
    mass_in,
    energy_in,
    width_in,
    e_out,
    l_out,
    beside,
    r2_ref,
    mx_ref,
    tot_ref,
    mom_ref,
    slope_ref,
    late,
    own,
    unit,
    near,
    dens_block,
    dens_dest,
    dens_near,
    position,
    velocity,
    mass,
    energy,
    first_width,
    ins,
    ys,
    yr,
    *sems,
):
    half = len(sems) // 2
    early_gather = Gather(own, e_out, True, *sems[:half])
    late_gather = Gather(late, l_out, False, *sems[half:])
    n = lax.axis_index("narrow")

    barrier = pltpu.get_barrier_semaphore()
    partners = [{"narrow": (n + k) % NY} for k in range(1, NY)]
    partners += [early_gather.device(0, 0, 1)]
    partners += [early_gather.device(0, k, 0) for k in range(1, NX)]
    partners += [early_gather.device(d, 0, 0) for d in Z_ORDER[1:] if abs(d) <= RELAY]
    for device in partners:
        pl.semaphore_signal(barrier, inc=1, device_id=device, device_id_type=MESH)

    incoming = [
        pltpu.make_async_copy(src, dst, ins.at[i])
        for i, (src, dst) in enumerate(
            (
                (near_in, near),
                (dens_block_in, dens_block),
                (dens_dest_in, dens_dest),
                (dens_near_in, dens_near),
                (position_in, position),
                (velocity_in, velocity),
                (mass_in, mass),
                (energy_in, energy),
                (width_in, first_width),
            )
        )
    ]
    for copy in incoming:
        copy.start()
    for copy in incoming:
        copy.wait()

    rows = lax.broadcasted_iota(jnp.int32, (NB, BLK), 0)
    for b in range(NB):
        for q in range(3):
            own[b, pl.ds(q, 1)] = position[pl.ds(q, 1), pl.ds(b * BLK, BLK)]
            own[b, pl.ds(3 + q, 1)] = velocity[pl.ds(q, 1), pl.ds(b * BLK, BLK)]
        own[b, pl.ds(6, 1)] = mass[pl.ds(b, 1)]
        own[b, pl.ds(7, 1)] = energy[pl.ds(b, 1)]
        unit[b] = jnp.where(rows == b, 1.0, 0.0)

    def set_slope(width):
        slope = -LOG2E / (width * width)
        for b in range(NB):
            slope_ref[b] = slope[b : b + 1]

    width = first_width[...]
    set_slope(width)

    def local_first(item, carry):
        target = own[item]
        first_sums(
            item,
            target,
            (target, own[near[item]]),
            slope_ref[item],
            r2_ref,
            mx_ref,
            tot_ref,
            mom_ref,
        )
        return carry

    lax.fori_loop(0, NB, local_first, 0, unroll=UNROLL_FIRST)
    beside[pl.ds(pl.multiple_of(n * NB, NB), NB)] = own[...]

    pl.semaphore_wait(barrier, len(partners))

    y_copies = []
    for k in range(1, NY):
        y_copies.append(
            remote(
                own,
                beside.at[pl.ds(pl.multiple_of(n * NB, NB), NB)],
                ys.at[NY - k],
                yr.at[NY - k],
                {"narrow": (n + k) % NY},
            )
        )
        y_copies[-1].start()
    early_gather.start()
    for copy in y_copies:
        copy.wait_recv()

    def export_first(e, carry):
        block = dens_block[e]
        first_sums(
            NB + e,
            own[block],
            tuple(beside[dens_dest[e] * NB + dens_near[s, e]] for s in range(2)),
            slope_ref[block],
            r2_ref,
            mx_ref,
            tot_ref,
            mom_ref,
        )
        return carry

    lax.fori_loop(0, XN, export_first, 0, unroll=UNROLL_FIRST)

    def follow(steps):
        for which, kind, batch in steps:
            gather = early_gather if which == "E" else late_gather
            {"z": gather.z_step, "n": gather.x_near, "f": gather.x_far}[kind](int(batch))

    def combined(ref):
        value = ref[pl.ds(0, NB)]
        for e in range(XN):
            value = value + unit[dens_block[e]] * ref[pl.ds(NB + e, 1)]
        return value

    follow(AFTER_FIRST_PASS)
    for step in range(PASSES):
        if step == PASSES - 1:
            follow(BEFORE_LAST_PASS)
        if step > 0:

            def local_next(item, carry):
                next_sums(item, slope_ref[item], r2_ref, mx_ref, tot_ref, mom_ref)
                return carry

            def export_next(e, carry):
                next_sums(NB + e, slope_ref[dens_block[e]], r2_ref, mx_ref, tot_ref, mom_ref)
                return carry

            lax.fori_loop(0, NB, local_next, 0, unroll=UNROLL_NEXT)
            lax.fori_loop(0, XN, export_next, 0, unroll=UNROLL_NEXT)
        total = combined(tot_ref)
        if step + 1 < PASSES:
            moment = combined(mom_ref)
            ratio = jnp.log(KERNEL_NORM * total / (TARGET_COUNT * mass[...]))
            bend = 2.0 * moment / (width * width * total)
            width = width * jnp.exp(-ratio / (3.0 + bend))
            set_slope(width)

    late[pl.ds(0, NB)] = width
    late[pl.ds(NB, NB)] = KERNEL_NORM * total / (width * width * width)
    late_gather.start()
    follow(AFTER_DENSITY)
    early_gather.finish()
    late_gather.finish()
    for copy in y_copies:
        copy.wait_send()


def gather_call(*args):
    batches = len(BATCHES)
    dma = pltpu.SemaphoreType.DMA
    per_gather = [dma((NZ + 1,)), dma((NZ + 1,))] + [dma((NX, batches))] * 4 + [dma]
    return pl.pallas_call(
        gather_kernel,
        out_shape=(
            jax.ShapeDtypeStruct((NC, NX, NZ, NB, 8, BLK), F32),
            jax.ShapeDtypeStruct((NC, NX, NZ, 2 * NB, BLK), F32),
        ),
        in_specs=[pl.BlockSpec(memory_space=pl.ANY)] * 9,
        out_specs=(pl.BlockSpec(memory_space=pl.ANY),) * 2,
        scratch_shapes=[
            pltpu.VMEM((NY * NB, 8, BLK), F32),
            pltpu.VMEM((NB + XN, 2 * BLK, BLK), F32),
            pltpu.VMEM((NB + XN, 2 * BLK, BLK), F32),
            pltpu.VMEM((NB + XN, BLK), F32),
            pltpu.VMEM((NB + XN, BLK), F32),
            pltpu.VMEM((NB, 1, BLK), F32),
            pltpu.VMEM((2 * NB, BLK), F32),
            pltpu.VMEM((NB, 8, BLK), F32),
            pltpu.VMEM((NB, NB, BLK), F32),
            pltpu.SMEM((NB,), jnp.int32),
            pltpu.SMEM((XN,), jnp.int32),
            pltpu.SMEM((XN,), jnp.int32),
            pltpu.SMEM((2, XN), jnp.int32),
            pltpu.VMEM((3, NB * BLK), F32),
            pltpu.VMEM((3, NB * BLK), F32),
            pltpu.VMEM((NB, BLK), F32),
            pltpu.VMEM((NB, BLK), F32),
            pltpu.VMEM((NB, BLK), F32),
            dma((9,)),
            dma((NY,)),
            dma((NY,)),
        ]
        + per_gather * 2,
        compiler_params=pltpu.CompilerParams(
            collective_id=0, has_side_effects=True, vmem_limit_bytes=62 * 2**20
        ),
        name="density_and_gather",
    )(*args)


def split_two(value):
    high = value.astype(BF16).astype(F32)
    return high, value - high


def split_three(value):
    high, rest = split_two(value)
    return (high,) + split_two(rest)


def target_features(tile, exp_i, scale_i):
    row = lax.broadcasted_iota(jnp.int32, tile.shape, 0)
    swapped = jnp.where(row < 3, pltpu.roll(tile, 5, 0), pltpu.roll(tile, 3, 0))
    squares = jnp.sum(jnp.where(row < 3, tile * tile, 0.0), axis=0, keepdims=True)
    crosses = jnp.sum(jnp.where(row < 3, tile * swapped, 0.0), axis=0, keepdims=True)
    distance = jnp.where(row < 3, -2.0 * tile, jnp.where(row == 6, 1.0, 0.0))
    approach = jnp.where(row < 6, -40.0 * swapped, jnp.where(row == 7, 40.0, 0.0))
    outs = []
    for factor, constant in (
        (distance, squares),
        (approach, 40.0 * crosses),
        (distance * exp_i, squares * exp_i + scale_i),
    ):
        h, m, l = split_three(factor)
        ch, cm, cl = split_three(constant)
        constants = jnp.where(row == 0, ch, jnp.where(row == 1, cm, jnp.where(row == 2, cl, 0.0)))
        full = jnp.concatenate([h, m, l, h, m, h, constants] + [jnp.zeros_like(h)] * 9, axis=0)
        outs.append(full.T)
    return jnp.concatenate(outs, axis=0).astype(BF16)[:, :KF]


T_SQ, T_CROSS, T_EXP, T_SCALE, T_WIDTH, T_SOUND, T_RHO, T_PRESS = range(8)


def slot_table(tab_ref, slot, tiles_ref, late_ref):
    def column(q):
        return tiles_ref[slot, pl.ds(q, NB, stride=8)]

    x, y, z, vx, vy, vz = (column(q) for q in range(6))
    energy = column(7)
    width = late_ref[slot, pl.ds(0, NB)]
    rho = late_ref[slot, pl.ds(NB, NB)]
    tab_ref[slot, T_SQ] = x * x + y * y + z * z
    tab_ref[slot, T_CROSS] = x * vx + y * vy + z * vz
    tab_ref[slot, T_EXP] = -LOG2E / (width * width)
    tab_ref[slot, T_SCALE] = math.log2(2.0 * KERNEL_NORM) - 5.0 * jnp.log2(width)
    tab_ref[slot, T_WIDTH] = 0.05 * width
    tab_ref[slot, T_SOUND] = jnp.sqrt((10.0 / 9.0) * energy)
    tab_ref[slot, T_RHO] = 8.0 * rho
    tab_ref[slot, T_PRESS] = (2.0 / 3.0) * energy / rho


TARGET_VALUES = (T_WIDTH, T_SOUND, T_RHO, T_PRESS)


def force_kernel(
    near_in,
    force_block_in,
    force_dest_in,
    force_near_in,
    tiles_in,
    late_in,
    rho_out,
    acc_out,
    heat_out,
    tab_ref,
    tiles_ref,
    late_ref,
    tl_ref,
    tg_ref,
    acc_ref,
    r0,
    r1,
    f0,
    f1,
    w0,
    w1,
    f2,
    near,
    force_block,
    force_dest,
    force_near,
    lists_v,
    lists,
    ins,
    tile_sems,
    late_sems,
):
    chunk = tiles_ref.shape[0] // CHUNKS
    incoming = [
        pltpu.make_async_copy(src, dst, ins.at[i])
        for i, (src, dst) in enumerate(
            (
                (near_in, near),
                (force_block_in, force_block),
                (force_dest_in, force_dest),
                (force_near_in, force_near),
            )
        )
    ]
    for copy in incoming:
        copy.start()

    loads = []
    for k in range(CHUNKS):
        part = pl.ds(k * chunk, chunk)
        loads.append(
            (
                pltpu.make_async_copy(tiles_in.at[part], tiles_ref.at[part], tile_sems.at[k]),
                pltpu.make_async_copy(late_in.at[part], late_ref.at[part], late_sems.at[k]),
            )
        )

    def start_load(k):
        for copy in loads[k]:
            copy.start()

    start_load(0)
    w = lax.axis_index("wide")
    for copy in incoming:
        copy.wait()
    there = force_dest[...]
    dz = ((there >> 3) - (w >> 3)) & 15
    dn = NZ - dz
    spot = jnp.where(
        dz <= NZ // 2,
        jnp.where(dz <= RELAY, 2 * dz + 1, 2 * dz - 1),
        jnp.where(dn <= RELAY, 2 * dn + 2, 2 * dn),
    )
    spot = jnp.where(dz == 0, 0, jnp.where(dz == RELAY, 1, jnp.where(dn == RELAY, 2, spot)))
    slot = (((there ^ w) & 1) * NX + (((there >> 1) - (w >> 1)) & 3)) * NZ + spot
    lists_v[:, pl.ds(0, XW)] = jnp.concatenate(
        [force_block[...], slot * NB + force_near[...]], axis=0
    )
    lists_v[:, pl.ds(XW, XW)] = jnp.zeros((3, XW), jnp.int32)
    to_scalars = pltpu.make_async_copy(lists_v, lists, ins.at[4])
    to_scalars.start()
    for k in range(1, CHUNKS):
        start_load(k)

    def fill(slot, carry):
        slot_table(tab_ref, slot, tiles_ref, late_ref)
        return carry

    def fill_chunk(k):
        for copy in loads[k]:
            copy.wait()
        lax.fori_loop(k * chunk, (k + 1) * chunk, fill, 0, unroll=4)

    fill_chunk(0)

    def prepare(b, carry):
        tl_ref[b] = target_features(
            tiles_ref[0, pl.ds(pl.multiple_of(b * 8, 8), 8)],
            tab_ref[0, T_EXP, pl.ds(b, 1)],
            tab_ref[0, T_SCALE, pl.ds(b, 1)],
        )
        for i, q in enumerate(TARGET_VALUES):
            tg_ref[b, i] = jnp.broadcast_to(tab_ref[0, q, pl.ds(b, 1)], (BLK, BLK)).T
        acc_ref[b] = jnp.zeros((16, 3 * BLK), F32)
        return carry

    lax.fori_loop(0, NB, prepare, 0, unroll=4)
    for k in range(1, CHUNKS):
        fill_chunk(k)
    to_scalars.wait()
    for b in range(NB):
        lists[0, XW + b] = b
        lists[1, XW + b] = b
        lists[2, XW + b] = near[b]
    f1[...] = jnp.zeros(f1.shape, BF16)
    w1[...] = jnp.zeros(w1.shape, BF16)

    def pick(i, q):
        a, b = lists[1, i], lists[2, i]
        return jnp.concatenate(
            [tab_ref[a >> 3, q, pl.ds(a & 7, 1)], tab_ref[b >> 3, q, pl.ds(b & 7, 1)]], axis=1
        )

    def products(i, r_ref, f_ref):
        a, b = lists[1, i], lists[2, i]
        raw = jnp.concatenate(
            [
                tiles_ref[s >> 3, pl.ds(pl.multiple_of((s & 7) * 8, 8), 8)]
                for s in (a, b)
            ],
            axis=1,
        )
        row = lax.broadcasted_iota(jnp.int32, raw.shape, 0)
        cross = pick(i, T_CROSS)
        u = jnp.where(row < 6, raw, jnp.where(row == 6, pick(i, T_SQ), cross))
        h, m, l = split_three(u)
        feats = jnp.concatenate([h, h, h, m, m, l, jnp.ones_like(h), jnp.zeros_like(h)], axis=0)
        r_ref[...] = jnp.dot(tl_ref[lists[0, i]], feats.astype(BF16), preferred_element_type=F32)
        f = jnp.where(row == 6, 1.0, u) * raw[6:7]
        f_ref[...] = jnp.concatenate(split_two(f), axis=0).astype(BF16)

    def pairs(i, r_ref, w_ref):
        b = lists[0, i]
        width_j, sound_j, rho_j, press_j = (pick(i, q) for q in TARGET_VALUES)
        exp_j, scale_j = pick(i, T_EXP), pick(i, T_SCALE)
        for g in range(8):
            r2 = r_ref[pl.ds(16 * g, 16)]
            vd = r_ref[pl.ds(BLK + 16 * g, 16)]

            def own(q):
                value = tg_ref[b, q, pl.ds(16 * g, 16)]
                return jnp.concatenate([value, value], axis=1)

            hs = own(0) + width_j
            nu = jnp.minimum(hs * vd * pl.reciprocal(r2 + hs * hs, approx=True), 0.0)
            visc = nu * (nu - (own(1) + sound_j)) * pl.reciprocal(own(2) + rho_j, approx=True)
            grad_i = jnp.exp2(r_ref[pl.ds(2 * BLK + 16 * g, 16)])
            grad_j = jnp.exp2(r2 * exp_j + scale_j)
            first = own(3) * grad_i
            both = first + visc * (grad_i + grad_j)
            w_ref[pl.ds(16 * g, 16)] = both.astype(BF16)
            w_ref[pl.ds(BLK + 16 * g, 16)] = first.astype(BF16)
            w_ref[pl.ds(2 * BLK + 16 * g, 16)] = (press_j * grad_j).astype(BF16)

    def reduce(i, f_ref, w_ref):
        b = lists[0, i]
        acc_ref[b] = acc_ref[b] + lax.dot_general(
            f_ref[...], w_ref[...], (((1,), (1,)), ((), ())), preferred_element_type=F32
        )

    products(0, r0, f0)

    def body(k, carry):
        i = 2 * k
        reduce(jnp.maximum(i - 1, 0), f1, w1)
        products(i + 1, r1, f1)
        pairs(i, r0, w0)
        products(jnp.minimum(i + 2, ITEMS - 1), r0, f2)
        reduce(i, f0, w0)
        f0[...] = f2[...]
        pairs(i + 1, r1, w1)
        return carry

    lax.fori_loop(0, ITEMS // 2, body, 0, unroll=17)
    reduce(ITEMS - 1, f1, w1)

    rho_out[...] = late_ref[0, pl.ds(NB, NB)]
    for b in range(NB):
        tile = tiles_ref[0, pl.ds(8 * b, 8)]
        s = acc_ref[b]
        s = s[0:8] + s[8:16]
        push, heat = s[:, 0:BLK] + s[:, 2 * BLK :], s[:, 0:BLK] + s[:, BLK : 2 * BLK]
        for q in range(3):
            acc_out[pl.ds(q, 1), pl.ds(b * BLK, BLK)] = tile[q : q + 1] * push[6:7] - push[q : q + 1]
        value = tab_ref[0, T_CROSS, pl.ds(b, 1)] * heat[6:7] + heat[7:8]
        for q in range(3):
            value = value - tile[3 + q : 4 + q] * heat[q : q + 1]
            value = value - tile[q : q + 1] * heat[3 + q : 4 + q]
        heat_out[pl.ds(b, 1)] = -0.5 * value


def force_call(*args):
    vmem = pl.BlockSpec(memory_space=pltpu.VMEM)
    slots = NC * NX * NZ
    return pl.pallas_call(
        force_kernel,
        out_shape=(
            jax.ShapeDtypeStruct((NB, BLK), F32),
            jax.ShapeDtypeStruct((3, NB * BLK), F32),
            jax.ShapeDtypeStruct((NB, BLK), F32),
        ),
        in_specs=[pl.BlockSpec(memory_space=pl.ANY)] * 6,
        out_specs=(vmem,) * 3,
        scratch_shapes=[
            pltpu.VMEM((slots, 8, NB, BLK), F32),
            pltpu.VMEM((slots, 8 * NB, BLK), F32),
            pltpu.VMEM((slots, 2 * NB, BLK), F32),
            pltpu.VMEM((NB, 3 * BLK, KF), BF16),
            pltpu.VMEM((NB, len(TARGET_VALUES), BLK, BLK), F32),
            pltpu.VMEM((NB, 16, 3 * BLK), F32),
            pltpu.VMEM((3 * BLK, 2 * BLK), F32),
            pltpu.VMEM((3 * BLK, 2 * BLK), F32),
            pltpu.VMEM((16, 2 * BLK), BF16),
            pltpu.VMEM((16, 2 * BLK), BF16),
            pltpu.VMEM((3 * BLK, 2 * BLK), BF16),
            pltpu.VMEM((3 * BLK, 2 * BLK), BF16),
            pltpu.VMEM((16, 2 * BLK), BF16),
            pltpu.SMEM((NB,), jnp.int32),
            pltpu.VMEM((1, XW), jnp.int32),
            pltpu.VMEM((1, XW), jnp.int32),
            pltpu.VMEM((2, XW), jnp.int32),
            pltpu.VMEM((3, 2 * XW), jnp.int32),
            pltpu.SMEM((3, 2 * XW), jnp.int32),
            pltpu.SemaphoreType.DMA((5,)),
            pltpu.SemaphoreType.DMA((CHUNKS,)),
            pltpu.SemaphoreType.DMA((CHUNKS,)),
        ],
        compiler_params=pltpu.CompilerParams(vmem_limit_bytes=62 * 2**20),
        name="force",
    )(*args)


def on_device(
    position,
    velocity,
    mass,
    energy,
    smoothing,
    local_near,
    dens_block,
    dens_dest,
    dens_near,
    force_block,
    force_dest,
    force_near,
):
    tiles, late = gather_call(
        local_near,
        dens_block,
        dens_dest.reshape(-1),
        dens_near.T,
        position,
        velocity,
        mass.reshape(NB, BLK),
        energy.reshape(NB, BLK),
        smoothing.reshape(NB, BLK),
    )
    slots = NC * NX * NZ
    rho, accel, heat = force_call(
        local_near,
        force_block.reshape(1, XW),
        force_dest.T,
        force_near.T,
        tiles.reshape(slots, 8 * NB, BLK),
        late.reshape(slots, 2 * NB, BLK),
    )
    return rho.reshape(NB * BLK), accel, heat.reshape(NB * BLK)


def solution(mesh):
    both = ("wide", "narrow")
    in_specs = (
        P(None, both),
        P(None, both),
        P(both),
        P(both),
        P(both),
        P(both),
        P(both),
        P(both, None),
        P(both, None),
        P(both),
        P(both, None),
        P(both, None),
    )
    out_specs = (P(both), P(None, both), P(both))
    return jax.shard_map(
        on_device, mesh=mesh, in_specs=in_specs, out_specs=out_specs, check_vma=False
    )
```

```python
import functools
import math

import jax
import jax.numpy as jnp
from jax import lax
from jax.experimental import pallas as pl
from jax.experimental.pallas import tpu as pltpu
from jax.sharding import PartitionSpec as P

F32, BF16 = jnp.float32, jnp.bfloat16
MESH = pl.DeviceIdType.MESH

PASSES = 3
KERNEL_NORM = math.pi ** (-1.5)
TARGET_COUNT = 24.0
LOG2E = math.log2(math.e)

NB = 8
BLK = 128
NZ, NX, NC, NY = 16, 4, 2, 4
XN = 8
XW = 128
ITEMS = NB + XW
CHUNKS = 8
KF = 64

RELAY = 4
Z_ORDER = [0, 4, -4, 1, -1, 2, -2, 3, -3, 5, -5, 6, -6, 7, -7, 8]
Z_PLACE = {d % NZ: p for p, d in enumerate(Z_ORDER)}
BATCHES = ((0, 1), (1, 5), (5, 9), (9, 13), (13, 16))
FAR = Z_PLACE[NZ // 2]


def remote(src, dst, send, recv, device):
    return pltpu.make_async_remote_copy(
        src_ref=src,
        dst_ref=dst,
        send_sem=send,
        recv_sem=recv,
        device_id=device,
        device_id_type=MESH,
    )


AFTER_FIRST_PASS = ("Ez1",)
BEFORE_LAST_PASS = ("En0",)
AFTER_DENSITY = (
    "Ez2", "En1", "Ef0", "Ez3", "Ez4", "En2", "Ef1", "En3",
    "Lz1", "Lz2", "Ef2", "En4", "Ln0", "Lf0", "Lz3", "Lz4",
    "Ef3", "Ln1", "Lf1", "Ef4", "Ln2", "Lf2", "Ln3", "Lf3",
    "Ln4", "Lf4",
)


UNROLL_FIRST = 4
UNROLL_NEXT = 8


class Gather:
    def __init__(self, own, out, halved, zs, zr, xs, xr, cs, cr, lsem):
        self.own, self.out, self.halved = own, out, halved
        self.zs, self.zr, self.xs, self.xr, self.cs, self.cr = zs, zr, xs, xr, cs, cr
        self.lsem = lsem
        w = lax.axis_index("wide")
        self.z, self.x, self.c = w // (NX * NC), (w // NC) % NX, w % NC
        self.half = own.shape[0] // 2
        self.sent = []

    def device(self, dz, dx, dc):
        z = (self.z + dz + NZ) % NZ
        x = (self.x + dx + NX) % NX
        c = (self.c + dc) % NC
        return {"wide": (z * NX + x) * NC + c}

    def go(self, copy):
        copy.start()
        self.sent.append(copy)

    def halves(self, ref, side):
        return ref.at[pl.ds(side * self.half, self.half)]

    def z_copy(self, src, distance, hop, side=None):
        place = Z_PLACE[distance % NZ]
        dst, sem = self.out.at[0, 0, place], place
        if side is not None:
            src, dst = self.halves(src, side), self.halves(dst, side)
            sem = place + side
        return remote(src, dst, self.zs.at[sem], self.zr.at[sem], self.device(hop, 0, 0))

    def start(self):
        self.local = pltpu.make_async_copy(self.own, self.out.at[0, 0, 0], self.lsem)
        self.local.start()
        for d in Z_ORDER[1:]:
            if abs(d) <= RELAY:
                self.go(self.z_copy(self.own, -d, d))
        self.local.wait()
        self.forward_x(0)
        self.forward_core(0, 0)

    def wait_z(self, batch):
        for place in range(*BATCHES[batch]):
            if place == FAR:
                for side in range(2):
                    self.z_copy(self.own, NZ // 2, 1, side).wait_recv()
            elif place > 0:
                self.z_copy(self.own, Z_ORDER[place], 1).wait_recv()

    def relay_z(self):
        for sign, side in ((1, 0), (-1, 1)):
            src = self.out.at[0, 0, Z_PLACE[-sign * RELAY % NZ]]
            for k in range(1, NZ // 2 - RELAY):
                self.go(self.z_copy(src, -sign * (RELAY + k), sign * k))
            self.go(self.z_copy(src, NZ // 2, sign * (NZ // 2 - RELAY), side))

    def part(self, core, x, batch, side=None):
        lo, hi = BATCHES[batch]
        if side is None:
            return self.out.at[core, x, pl.ds(lo, hi - lo)]
        return self.out.at[core, x, pl.ds(lo, hi - lo), pl.ds(side * self.half, self.half)]

    def x_copy(self, batch, k):
        j = NX - k
        return remote(
            self.part(0, 0, batch),
            self.part(0, j, batch),
            self.xs.at[j, batch],
            self.xr.at[j, batch],
            self.device(0, k, 0),
        )

    def x_relay(self, batch, side):
        sign = 1 - 2 * side
        sem = 2 * side
        return remote(
            self.part(0, (NX - sign) % NX, batch, side),
            self.part(0, 2, batch, side),
            self.xs.at[sem, batch],
            self.xr.at[sem, batch],
            self.device(0, sign, 0),
        )

    def forward_x(self, batch):
        for k in (1, 3) if self.halved else (2, 1, 3):
            self.go(self.x_copy(batch, k))

    def core_copy(self, x, batch):
        return remote(
            self.part(0, x, batch),
            self.part(1, x, batch),
            self.cs.at[x, batch],
            self.cr.at[x, batch],
            self.device(0, 0, 1),
        )

    def forward_core(self, x, batch):
        self.go(self.core_copy(x, batch))

    def z_step(self, batch):
        self.wait_z(batch)
        if batch == 1:
            self.relay_z()
        self.forward_x(batch)
        self.forward_core(0, batch)

    def x_near(self, batch):
        for k, side in ((1, 0), (3, 1)):
            self.x_copy(batch, k).wait_recv()
            if self.halved:
                self.go(self.x_relay(batch, side))
        self.forward_core(1, batch)
        self.forward_core(3, batch)

    def x_far(self, batch):
        if self.halved:
            for side in range(2):
                self.x_relay(batch, side).wait_recv()
        else:
            self.x_copy(batch, 2).wait_recv()
        self.forward_core(2, batch)

    def finish(self):
        for batch in range(len(BATCHES)):
            for x in range(NX):
                self.core_copy(x, batch).wait_recv()
        for copy in self.sent:
            copy.wait_send()


def first_sums(item, target, sources, slope, r2_ref, mx_ref, tot_ref, mom_ref):
    tot = mom = 0.0
    for s, source in enumerate(sources):
        cols = source.T
        r2 = 0.0
        for q in range(3):
            delta = target[q : q + 1] - cols[:, q : q + 1]
            r2 = r2 + delta * delta
        mass = jnp.broadcast_to(cols[:, 6:7], (BLK, BLK))
        r2_ref[item, pl.ds(s * BLK, BLK)] = r2
        mx_ref[item, pl.ds(s * BLK, BLK)] = mass
        weight = jnp.exp2(r2 * slope) * mass
        tot = tot + jnp.sum(weight, axis=0, keepdims=True)
        mom = mom + jnp.sum(weight * r2, axis=0, keepdims=True)
    tot_ref[pl.ds(item, 1)] = tot
    mom_ref[pl.ds(item, 1)] = mom


def next_sums(item, slope, r2_ref, mx_ref, tot_ref, mom_ref):
    r2 = r2_ref[item]
    weight = jnp.exp2(r2 * slope) * mx_ref[item]
    tot_ref[pl.ds(item, 1)] = jnp.sum(weight, axis=0, keepdims=True)
    mom_ref[pl.ds(item, 1)] = jnp.sum(weight * r2, axis=0, keepdims=True)


def gather_kernel(
    near_in,
    dens_block_in,
    dens_dest_in,
    dens_near_in,
    position_in,
    velocity_in,
    mass_in,
    energy_in,
    width_in,
    e_out,
    l_out,
    beside,
    r2_ref,
    mx_ref,
    tot_ref,
    mom_ref,
    slope_ref,
    late,
    own,
    unit,
    near,
    dens_block,
    dens_dest,
    dens_near,
    position,
    velocity,
    mass,
    energy,
    first_width,
    ins,
    ys,
    yr,
    *sems,
):
    half = len(sems) // 2
    early_gather = Gather(own, e_out, True, *sems[:half])
    late_gather = Gather(late, l_out, False, *sems[half:])
    n = lax.axis_index("narrow")

    barrier = pltpu.get_barrier_semaphore()
    partners = [{"narrow": (n + k) % NY} for k in range(1, NY)]
    partners += [early_gather.device(0, 0, 1)]
    partners += [early_gather.device(0, k, 0) for k in range(1, NX)]
    partners += [early_gather.device(d, 0, 0) for d in Z_ORDER[1:] if abs(d) <= RELAY]
    for device in partners:
        pl.semaphore_signal(barrier, inc=1, device_id=device, device_id_type=MESH)

    incoming = [
        pltpu.make_async_copy(src, dst, ins.at[i])
        for i, (src, dst) in enumerate(
            (
                (near_in, near),
                (dens_block_in, dens_block),
                (dens_dest_in, dens_dest),
                (dens_near_in, dens_near),
                (position_in, position),
                (velocity_in, velocity),
                (mass_in, mass),
                (energy_in, energy),
                (width_in, first_width),
            )
        )
    ]
    for copy in incoming:
        copy.start()
    for copy in incoming:
        copy.wait()

    rows = lax.broadcasted_iota(jnp.int32, (NB, BLK), 0)
    for b in range(NB):
        for q in range(3):
            own[b, pl.ds(q, 1)] = position[pl.ds(q, 1), pl.ds(b * BLK, BLK)]
            own[b, pl.ds(3 + q, 1)] = velocity[pl.ds(q, 1), pl.ds(b * BLK, BLK)]
        own[b, pl.ds(6, 1)] = mass[pl.ds(b, 1)]
        own[b, pl.ds(7, 1)] = energy[pl.ds(b, 1)]
        unit[b] = jnp.where(rows == b, 1.0, 0.0)

    def set_slope(width):
        slope = -LOG2E / (width * width)
        for b in range(NB):
            slope_ref[b] = slope[b : b + 1]

    width = first_width[...]
    set_slope(width)

    def local_first(item, carry):
        target = own[item]
        first_sums(
            item,
            target,
            (target, own[near[item]]),
            slope_ref[item],
            r2_ref,
            mx_ref,
            tot_ref,
            mom_ref,
        )
        return carry

    lax.fori_loop(0, NB, local_first, 0, unroll=UNROLL_FIRST)
    beside[pl.ds(pl.multiple_of(n * NB, NB), NB)] = own[...]

    pl.semaphore_wait(barrier, len(partners))

    y_copies = []
    for k in range(1, NY):
        y_copies.append(
            remote(
                own,
                beside.at[pl.ds(pl.multiple_of(n * NB, NB), NB)],
                ys.at[NY - k],
                yr.at[NY - k],
                {"narrow": (n + k) % NY},
            )
        )
        y_copies[-1].start()
    early_gather.start()
    for copy in y_copies:
        copy.wait_recv()

    def export_first(e, carry):
        block = dens_block[e]
        first_sums(
            NB + e,
            own[block],
            tuple(beside[dens_dest[e] * NB + dens_near[s, e]] for s in range(2)),
            slope_ref[block],
            r2_ref,
            mx_ref,
            tot_ref,
            mom_ref,
        )
        return carry

    lax.fori_loop(0, XN, export_first, 0, unroll=UNROLL_FIRST)

    def follow(steps):
        for which, kind, batch in steps:
            gather = early_gather if which == "E" else late_gather
            {"z": gather.z_step, "n": gather.x_near, "f": gather.x_far}[kind](int(batch))

    def combined(ref):
        value = ref[pl.ds(0, NB)]
        for e in range(XN):
            value = value + unit[dens_block[e]] * ref[pl.ds(NB + e, 1)]
        return value

    follow(AFTER_FIRST_PASS)
    for step in range(PASSES):
        if step == PASSES - 1:
            follow(BEFORE_LAST_PASS)
        if step > 0:

            def local_next(item, carry):
                next_sums(item, slope_ref[item], r2_ref, mx_ref, tot_ref, mom_ref)
                return carry

            def export_next(e, carry):
                next_sums(NB + e, slope_ref[dens_block[e]], r2_ref, mx_ref, tot_ref, mom_ref)
                return carry

            lax.fori_loop(0, NB, local_next, 0, unroll=UNROLL_NEXT)
            lax.fori_loop(0, XN, export_next, 0, unroll=UNROLL_NEXT)
        total = combined(tot_ref)
        if step + 1 < PASSES:
            moment = combined(mom_ref)
            ratio = jnp.log(KERNEL_NORM * total / (TARGET_COUNT * mass[...]))
            bend = 2.0 * moment / (width * width * total)
            width = width * jnp.exp(-ratio / (3.0 + bend))
            set_slope(width)

    late[pl.ds(0, NB)] = width
    late[pl.ds(NB, NB)] = KERNEL_NORM * total / (width * width * width)
    late_gather.start()
    follow(AFTER_DENSITY)
    early_gather.finish()
    late_gather.finish()
    for copy in y_copies:
        copy.wait_send()


def gather_call(*args):
    batches = len(BATCHES)
    dma = pltpu.SemaphoreType.DMA
    per_gather = [dma((NZ + 1,)), dma((NZ + 1,))] + [dma((NX, batches))] * 4 + [dma]
    return pl.pallas_call(
        gather_kernel,
        out_shape=(
            jax.ShapeDtypeStruct((NC, NX, NZ, NB, 8, BLK), F32),
            jax.ShapeDtypeStruct((NC, NX, NZ, 2 * NB, BLK), F32),
        ),
        in_specs=[pl.BlockSpec(memory_space=pl.ANY)] * 9,
        out_specs=(pl.BlockSpec(memory_space=pl.ANY),) * 2,
        scratch_shapes=[
            pltpu.VMEM((NY * NB, 8, BLK), F32),
            pltpu.VMEM((NB + XN, 2 * BLK, BLK), F32),
            pltpu.VMEM((NB + XN, 2 * BLK, BLK), F32),
            pltpu.VMEM((NB + XN, BLK), F32),
            pltpu.VMEM((NB + XN, BLK), F32),
            pltpu.VMEM((NB, 1, BLK), F32),
            pltpu.VMEM((2 * NB, BLK), F32),
            pltpu.VMEM((NB, 8, BLK), F32),
            pltpu.VMEM((NB, NB, BLK), F32),
            pltpu.SMEM((NB,), jnp.int32),
            pltpu.SMEM((XN,), jnp.int32),
            pltpu.SMEM((XN,), jnp.int32),
            pltpu.SMEM((2, XN), jnp.int32),
            pltpu.VMEM((3, NB * BLK), F32),
            pltpu.VMEM((3, NB * BLK), F32),
            pltpu.VMEM((NB, BLK), F32),
            pltpu.VMEM((NB, BLK), F32),
            pltpu.VMEM((NB, BLK), F32),
            dma((9,)),
            dma((NY,)),
            dma((NY,)),
        ]
        + per_gather * 2,
        compiler_params=pltpu.CompilerParams(
            collective_id=0, has_side_effects=True, vmem_limit_bytes=62 * 2**20
        ),
        name="density_and_gather",
    )(*args)


def split_two(value):
    high = value.astype(BF16).astype(F32)
    return high, value - high


def split_three(value):
    high, rest = split_two(value)
    return (high,) + split_two(rest)


def target_features(tile, exp_i, scale_i):
    row = lax.broadcasted_iota(jnp.int32, tile.shape, 0)
    swapped = jnp.where(row < 3, pltpu.roll(tile, 5, 0), pltpu.roll(tile, 3, 0))
    squares = jnp.sum(jnp.where(row < 3, tile * tile, 0.0), axis=0, keepdims=True)
    crosses = jnp.sum(jnp.where(row < 3, tile * swapped, 0.0), axis=0, keepdims=True)
    distance = jnp.where(row < 3, -2.0 * tile, jnp.where(row == 6, 1.0, 0.0))
    approach = jnp.where(row < 6, -40.0 * swapped, jnp.where(row == 7, 40.0, 0.0))
    outs = []
    for factor, constant in (
        (distance, squares),
        (approach, 40.0 * crosses),
        (distance * exp_i, squares * exp_i + scale_i),
    ):
        h, m, l = split_three(factor)
        ch, cm, cl = split_three(constant)
        constants = jnp.where(row == 0, ch, jnp.where(row == 1, cm, jnp.where(row == 2, cl, 0.0)))
        full = jnp.concatenate([h, m, l, h, m, h, constants] + [jnp.zeros_like(h)] * 9, axis=0)
        outs.append(full.T)
    return jnp.concatenate(outs, axis=0).astype(BF16)[:, :KF]


T_SQ, T_CROSS, T_EXP, T_SCALE, T_WIDTH, T_SOUND, T_RHO, T_PRESS = range(8)


def slot_table(tab_ref, slot, tiles_ref, late_ref):
    def column(q):
        return tiles_ref[slot, pl.ds(q, NB, stride=8)]

    x, y, z, vx, vy, vz = (column(q) for q in range(6))
    energy = column(7)
    width = late_ref[slot, pl.ds(0, NB)]
    rho = late_ref[slot, pl.ds(NB, NB)]
    tab_ref[slot, T_SQ] = x * x + y * y + z * z
    tab_ref[slot, T_CROSS] = x * vx + y * vy + z * vz
    tab_ref[slot, T_EXP] = -LOG2E / (width * width)
    tab_ref[slot, T_SCALE] = math.log2(2.0 * KERNEL_NORM) - 5.0 * jnp.log2(width)
    tab_ref[slot, T_WIDTH] = 0.05 * width
    tab_ref[slot, T_SOUND] = jnp.sqrt((10.0 / 9.0) * energy)
    tab_ref[slot, T_RHO] = 8.0 * rho
    tab_ref[slot, T_PRESS] = (2.0 / 3.0) * energy / rho


TARGET_VALUES = (T_WIDTH, T_SOUND, T_RHO)


def force_kernel(
    near_in,
    force_block_in,
    force_dest_in,
    force_near_in,
    tiles_in,
    late_in,
    rho_out,
    acc_out,
    heat_out,
    tab_ref,
    tiles_ref,
    late_ref,
    tl_ref,
    tg_ref,
    acc_ref,
    r0,
    r1,
    f0,
    f1,
    w0,
    w1,
    f2,
    near,
    force_block,
    force_dest,
    force_near,
    lists_v,
    lists,
    ins,
    tile_sems,
    late_sems,
):
    chunk = tiles_ref.shape[0] // CHUNKS
    incoming = [
        pltpu.make_async_copy(src, dst, ins.at[i])
        for i, (src, dst) in enumerate(
            (
                (near_in, near),
                (force_block_in, force_block),
                (force_dest_in, force_dest),
                (force_near_in, force_near),
            )
        )
    ]
    for copy in incoming:
        copy.start()

    loads = []
    for k in range(CHUNKS):
        part = pl.ds(k * chunk, chunk)
        loads.append(
            (
                pltpu.make_async_copy(tiles_in.at[part], tiles_ref.at[part], tile_sems.at[k]),
                pltpu.make_async_copy(late_in.at[part], late_ref.at[part], late_sems.at[k]),
            )
        )

    def start_load(k):
        for copy in loads[k]:
            copy.start()

    start_load(0)
    w = lax.axis_index("wide")
    for copy in incoming:
        copy.wait()
    there = force_dest[...]
    dz = ((there >> 3) - (w >> 3)) & 15
    dn = NZ - dz
    spot = jnp.where(
        dz <= NZ // 2,
        jnp.where(dz <= RELAY, 2 * dz + 1, 2 * dz - 1),
        jnp.where(dn <= RELAY, 2 * dn + 2, 2 * dn),
    )
    spot = jnp.where(dz == 0, 0, jnp.where(dz == RELAY, 1, jnp.where(dn == RELAY, 2, spot)))
    slot = (((there ^ w) & 1) * NX + (((there >> 1) - (w >> 1)) & 3)) * NZ + spot
    lists_v[:, pl.ds(0, XW)] = jnp.concatenate(
        [force_block[...], slot * NB + force_near[...]], axis=0
    )
    lists_v[:, pl.ds(XW, XW)] = jnp.zeros((3, XW), jnp.int32)
    to_scalars = pltpu.make_async_copy(lists_v, lists, ins.at[4])
    to_scalars.start()
    for k in range(1, CHUNKS):
        start_load(k)

    def fill(slot, carry):
        slot_table(tab_ref, slot, tiles_ref, late_ref)
        return carry

    def fill_chunk(k):
        for copy in loads[k]:
            copy.wait()
        lax.fori_loop(k * chunk, (k + 1) * chunk, fill, 0, unroll=4)

    fill_chunk(0)

    def prepare(b, carry):
        tl_ref[b] = target_features(
            tiles_ref[0, pl.ds(pl.multiple_of(b * 8, 8), 8)],
            tab_ref[0, T_EXP, pl.ds(b, 1)],
            tab_ref[0, T_SCALE, pl.ds(b, 1)],
        )
        for i, q in enumerate(TARGET_VALUES):
            tg_ref[b, i] = jnp.broadcast_to(tab_ref[0, q, pl.ds(b, 1)], (BLK, BLK)).T
        acc_ref[b] = jnp.zeros((16, 3 * BLK), F32)
        return carry

    lax.fori_loop(0, NB, prepare, 0, unroll=4)
    for k in range(1, CHUNKS):
        fill_chunk(k)
    to_scalars.wait()
    for b in range(NB):
        lists[0, XW + b] = b
        lists[1, XW + b] = b
        lists[2, XW + b] = near[b]
    f1[...] = jnp.zeros(f1.shape, BF16)
    w1[...] = jnp.zeros(w1.shape, BF16)

    def pick(i, q):
        a, b = lists[1, i], lists[2, i]
        return jnp.concatenate(
            [tab_ref[a >> 3, q, pl.ds(a & 7, 1)], tab_ref[b >> 3, q, pl.ds(b & 7, 1)]], axis=1
        )

    def products(i, r_ref, f_ref):
        a, b = lists[1, i], lists[2, i]
        raw = jnp.concatenate(
            [
                tiles_ref[s >> 3, pl.ds(pl.multiple_of((s & 7) * 8, 8), 8)]
                for s in (a, b)
            ],
            axis=1,
        )
        row = lax.broadcasted_iota(jnp.int32, raw.shape, 0)
        cross = pick(i, T_CROSS)
        u = jnp.where(row < 6, raw, jnp.where(row == 6, pick(i, T_SQ), cross))
        h, m, l = split_three(u)
        feats = jnp.concatenate([h, h, h, m, m, l, jnp.ones_like(h), jnp.zeros_like(h)], axis=0)
        r_ref[...] = jnp.dot(tl_ref[lists[0, i]], feats.astype(BF16), preferred_element_type=F32)
        f = jnp.where(row == 6, 1.0, u) * raw[6:7]
        pressed = f * pick(i, T_PRESS)
        f_ref[...] = jnp.concatenate(split_two(f) + split_two(pressed), axis=0).astype(BF16)

    def pairs(i, r_ref, w_ref):
        b = lists[0, i]
        width_j, sound_j, rho_j = (pick(i, q) for q in TARGET_VALUES)
        exp_j, scale_j = pick(i, T_EXP), pick(i, T_SCALE)
        for g in range(8):
            r2 = r_ref[pl.ds(16 * g, 16)]
            vd = r_ref[pl.ds(BLK + 16 * g, 16)]

            def own(q):
                value = tg_ref[b, q, pl.ds(16 * g, 16)]
                return jnp.concatenate([value, value], axis=1)

            hs = own(0) + width_j
            nu = jnp.minimum(hs * vd * pl.reciprocal(r2 + hs * hs, approx=True), 0.0)
            visc = nu * (nu - (own(1) + sound_j)) * pl.reciprocal(own(2) + rho_j, approx=True)
            grad_i = jnp.exp2(r_ref[pl.ds(2 * BLK + 16 * g, 16)])
            grad_j = jnp.exp2(r2 * exp_j + scale_j)
            w_ref[pl.ds(16 * g, 16)] = (visc * (grad_i + grad_j)).astype(BF16)
            w_ref[pl.ds(BLK + 16 * g, 16)] = grad_i.astype(BF16)
            w_ref[pl.ds(2 * BLK + 16 * g, 16)] = grad_j.astype(BF16)

    def reduce(i, f_ref, w_ref):
        b = lists[0, i]
        for rows, cols in ((0, pl.ds(0, 2 * BLK)), (16, pl.ds(2 * BLK, BLK))):
            acc_ref[b, :, cols] = acc_ref[b, :, cols] + lax.dot_general(
                f_ref[pl.ds(rows, 16)],
                w_ref[cols],
                (((1,), (1,)), ((), ())),
                preferred_element_type=F32,
            )

    products(0, r0, f0)

    def body(k, carry):
        i = 2 * k
        reduce(jnp.maximum(i - 1, 0), f1, w1)
        products(i + 1, r1, f1)
        pairs(i, r0, w0)
        products(jnp.minimum(i + 2, ITEMS - 1), r0, f2)
        reduce(i, f0, w0)
        f0[...] = f2[...]
        pairs(i + 1, r1, w1)
        return carry

    lax.fori_loop(0, ITEMS // 2, body, 0, unroll=34)
    reduce(ITEMS - 1, f1, w1)

    rho_out[...] = late_ref[0, pl.ds(NB, NB)]
    for b in range(NB):
        tile = tiles_ref[0, pl.ds(8 * b, 8)]
        s = acc_ref[b]
        s = s[0:8] + s[8:16]
        visc, first = s[:, 0:BLK], tab_ref[0, T_PRESS, pl.ds(b, 1)] * s[:, BLK : 2 * BLK]
        push, heat = first + visc + s[:, 2 * BLK :], 2.0 * first + visc
        for q in range(3):
            acc_out[pl.ds(q, 1), pl.ds(b * BLK, BLK)] = tile[q : q + 1] * push[6:7] - push[q : q + 1]
        value = tab_ref[0, T_CROSS, pl.ds(b, 1)] * heat[6:7] + heat[7:8]
        for q in range(3):
            value = value - tile[3 + q : 4 + q] * heat[q : q + 1]
            value = value - tile[q : q + 1] * heat[3 + q : 4 + q]
        heat_out[pl.ds(b, 1)] = -0.5 * value


def force_call(*args):
    vmem = pl.BlockSpec(memory_space=pltpu.VMEM)
    slots = NC * NX * NZ
    return pl.pallas_call(
        force_kernel,
        out_shape=(
            jax.ShapeDtypeStruct((NB, BLK), F32),
            jax.ShapeDtypeStruct((3, NB * BLK), F32),
            jax.ShapeDtypeStruct((NB, BLK), F32),
        ),
        in_specs=[pl.BlockSpec(memory_space=pl.ANY)] * 6,
        out_specs=(vmem,) * 3,
        scratch_shapes=[
            pltpu.VMEM((slots, 8, NB, BLK), F32),
            pltpu.VMEM((slots, 8 * NB, BLK), F32),
            pltpu.VMEM((slots, 2 * NB, BLK), F32),
            pltpu.VMEM((NB, 3 * BLK, KF), BF16),
            pltpu.VMEM((NB, len(TARGET_VALUES), BLK, BLK), F32),
            pltpu.VMEM((NB, 16, 3 * BLK), F32),
            pltpu.VMEM((3 * BLK, 2 * BLK), F32),
            pltpu.VMEM((3 * BLK, 2 * BLK), F32),
            pltpu.VMEM((32, 2 * BLK), BF16),
            pltpu.VMEM((32, 2 * BLK), BF16),
            pltpu.VMEM((3 * BLK, 2 * BLK), BF16),
            pltpu.VMEM((3 * BLK, 2 * BLK), BF16),
            pltpu.VMEM((32, 2 * BLK), BF16),
            pltpu.SMEM((NB,), jnp.int32),
            pltpu.VMEM((1, XW), jnp.int32),
            pltpu.VMEM((1, XW), jnp.int32),
            pltpu.VMEM((2, XW), jnp.int32),
            pltpu.VMEM((3, 2 * XW), jnp.int32),
            pltpu.SMEM((3, 2 * XW), jnp.int32),
            pltpu.SemaphoreType.DMA((5,)),
            pltpu.SemaphoreType.DMA((CHUNKS,)),
            pltpu.SemaphoreType.DMA((CHUNKS,)),
        ],
        compiler_params=pltpu.CompilerParams(vmem_limit_bytes=62 * 2**20),
        name="force",
    )(*args)


def on_device(
    position,
    velocity,
    mass,
    energy,
    smoothing,
    local_near,
    dens_block,
    dens_dest,
    dens_near,
    force_block,
    force_dest,
    force_near,
):
    tiles, late = gather_call(
        local_near,
        dens_block,
        dens_dest.reshape(-1),
        dens_near.T,
        position,
        velocity,
        mass.reshape(NB, BLK),
        energy.reshape(NB, BLK),
        smoothing.reshape(NB, BLK),
    )
    slots = NC * NX * NZ
    rho, accel, heat = force_call(
        local_near,
        force_block.reshape(1, XW),
        force_dest.T,
        force_near.T,
        tiles.reshape(slots, 8 * NB, BLK),
        late.reshape(slots, 2 * NB, BLK),
    )
    return rho.reshape(NB * BLK), accel, heat.reshape(NB * BLK)


def solution(mesh):
    both = ("wide", "narrow")
    in_specs = (
        P(None, both),
        P(None, both),
        P(both),
        P(both),
        P(both),
        P(both),
        P(both),
        P(both, None),
        P(both, None),
        P(both),
        P(both, None),
        P(both, None),
    )
    out_specs = (P(both), P(None, both), P(both))
    return jax.shard_map(
        on_device, mesh=mesh, in_specs=in_specs, out_specs=out_specs, check_vma=False
    )
```
